32 devices in a mesh: rows: 8 (over z, y), cols: 4 (over x, core).
Axes of the slice: x: 2, y: 2, z: 4, core: 2. Of those that a mesh axis runs over, the one named last changes fastest.
Arguments:
- l_blocks: bfloat16 [256, 64, 1920], P(('rows', 'cols')), may hold values from -0.25 to 0.25
- s_blocks: bfloat16 [256, 64, 1280], P('rows', None, 'cols'), may hold values from -6 to 6
- l_index: int32 [256, 30], P(('rows', 'cols')), may hold values from 0 to 255, as said below
- s_cols: int32 [256, 20], replicated, may hold values from 0 to 255, as said below
- c_index: int32 [256, 24], P(('rows', 'cols')), may hold values from 0 to 255, as said below
Outputs:
- product: bfloat16 [256, 64, 1536], P(('rows', 'cols'))
The draws below stay inside these ranges and needn't reach their ends.
Inputs may be any that keep to these rules, and one draw needn't show every extreme that they name: `l_index`: the 30 entries of block-row i are distinct and lie in the window of 31 block-rows starting at max(0, min(i - 15, 225)). `s_cols`: the entries of one block-row are distinct; those in slots p * 5 to (p + 1) * 5 - 1 are congruent to p modulo 20 // 5 and lie within 7 such columns around the block-row. `c_index`: the entries of one block-row are distinct; those in slots p * 6 to (p + 1) * 6 - 1 are congruent to p modulo 24 // 6 and lie within 16 such columns around the block-row.
All inputs are finite; a program needn't handle non-finite values.
Results may differ from the reference program's by a relative error of at most 0.001.
Values may be sent and summed in bfloat16 or wider, within the bound.
A program may use at most 192 MiB of HBM per device.

```python
import math
import jax
import jax.numpy as jnp
from jax import lax

B = 64
KL = 30
KS = 20
KC = 24
HL = 15
SW = 7
CW = 16
NB = 256
KSP = 5
KCP = 6


def pick_distinct(key, count, span, keep):
    scores = jax.random.randint(key, (count, span), 0, 1 << 20) * span + jnp.arange(span, dtype=jnp.int32)[None, :]
    order = jnp.argsort(scores, axis=1)
    return jnp.sort(order[:, :keep], axis=1).astype(jnp.int32)


def partition_cols(key, keep, span, nparts):
    per_part = NB // nparts
    positions = jnp.arange(NB, dtype=jnp.int32)
    start = jnp.clip(positions // nparts - span // 2, 0, per_part - span)
    pieces = []
    for part_id in range(nparts):
        chosen = pick_distinct(jax.random.fold_in(key, part_id + 11), NB, span, keep)
        pieces.append(nparts * (start[:, None] + chosen) + part_id)
    return jnp.concatenate(pieces, axis=1).astype(jnp.int32)


def draw_l_index(key, part):
    span = 2 * HL + 1
    positions = jnp.arange(NB, dtype=jnp.int32)
    start = jnp.clip(positions - HL, 0, NB - span)
    return (start[:, None] + pick_distinct(jax.random.fold_in(key, 3), NB, span, KL)).astype(jnp.int32)


def draw_s_cols(key, part):
    return partition_cols(jax.random.fold_in(key, 5), KSP, SW, KS // KSP)


def draw_c_index(key, part):
    return partition_cols(jax.random.fold_in(key, 7), KCP, CW, KC // KCP)


def block_levels(key, extent, cuts, least, largest):
    factor_of = 1.0
    for dim, blocks in cuts:
        steps = jax.random.uniform(jax.random.fold_in(jax.random.fold_in(key, 6), dim), (blocks,), jnp.float32, least / len(cuts), largest / len(cuts))
        factor_of = factor_of * jnp.repeat(jnp.exp(steps), extent[dim] // blocks).reshape((-1,) + (1,) * (len(extent) - 1 - dim))
    return factor_of


def bell_draw(key, shape, spread, most, cuts=(), kind=jnp.bfloat16):
    entries = spread * jax.random.normal(key, shape, jnp.float32)
    if cuts:
        entries = entries * block_levels(key, shape, cuts, -0.22, 0.18)
    return jnp.clip(entries, -most, most).astype(kind)


def setup_inputs(seed: int = 0) -> dict:
    arg_keys = jax.random.split(jax.random.key(seed), 6)
    l_blocks = bell_draw(arg_keys[0], (NB, B, KL * B), (9 * B) ** -0.5, 0.25, ((0, 32),))
    s_blocks = bell_draw(arg_keys[1], (NB, B, KS * B), 1.0, 6.0, ((0, 8), (2, 4)))
    l_index = draw_l_index(jax.random.fold_in(arg_keys[5], 71), 0)
    s_cols = draw_s_cols(jax.random.fold_in(arg_keys[5], 71), 0)
    c_index = draw_c_index(jax.random.fold_in(arg_keys[5], 71), 0)
    return dict(l_blocks=l_blocks, s_blocks=s_blocks, l_index=l_index, s_cols=s_cols, c_index=c_index)


def block_row(left_row, left_ids, want_cols, s_four, s_cols):
    width = s_four.shape[1]
    slot_total = s_four.shape[2]
    slot_ids = jnp.take(s_cols, left_ids, axis=0)
    match = slot_ids[:, None, :] == want_cols[None, :, None]
    slot_pick = jnp.sum(jnp.where(match, lax.iota(jnp.int32, slot_total)[None, None, :], 0), axis=2, dtype=jnp.int32)
    found = jnp.any(match, axis=2)
    picked = s_four[left_ids.astype(jnp.int32)[:, None], :, slot_pick, :]
    picked = jnp.where(found[:, :, None, None], picked.astype(jnp.float32), jnp.float32(0.0))
    left_three = left_row.reshape(width, left_ids.shape[0], width).astype(jnp.float32)
    summed = jnp.einsum('akb,kmbc->amc', left_three, picked, precision=lax.Precision.HIGHEST)
    return summed.reshape(width, want_cols.shape[0] * width).astype(jnp.bfloat16)


def reference(l_blocks, s_blocks, l_index, s_cols, c_index):
    total = l_blocks.shape[0]
    width = l_blocks.shape[1]
    s_four = s_blocks.reshape(total, width, s_blocks.shape[2] // width, width)
    per_turn = math.gcd(total, 8)

    def single(left_row, left_ids, want_cols):
        return block_row(left_row, left_ids, want_cols, s_four, s_cols)

    def one_group(group):
        return jax.vmap(single)(group[0], group[1], group[2])

    shaped = tuple(a.reshape((total // per_turn, per_turn) + a.shape[1:]) for a in (l_blocks, l_index, c_index))
    result = lax.map(one_group, shaped)
    return result.reshape((total,) + result.shape[2:])
```

```python
import functools

import jax
import jax.numpy as jnp
from jax import lax
from jax.experimental import pallas as pl
from jax.experimental.pallas import tpu as pltpu
from jax.sharding import PartitionSpec as P

MESH = pl.DeviceIdType.MESH
B = 64
PARTS = 4
KSP = 5
SPAN = 7
TILES = 20
CHUNKS = 6
QUADS = 16
VIEW = 5
ZERO_S = 160
X0, A0, C0, E0, D0, F0, G0 = 0, 4, 8, 10, 12, 16, 18


def place(row_count):
    r = lax.axis_index("rows")
    c = lax.axis_index("cols")
    x = c // 2
    outer = jnp.where(x == 0, (c == 0) & (r > 0), (c == 3) & (r < row_count - 1))
    skip = jnp.where(x == 0, jnp.where(outer, 0, 1), jnp.where(outer, 1, 0))
    first_quad = 8 * r - 4 * (1 - x) + 2 * skip
    return r, c, x, outer, skip, first_quad


def swap(v):
    return jnp.concatenate([v[:, B:], v[:, :B]], axis=1)


def kernel(
    row_count, s_ref, l_ref, t_ref, lt_ref, ct_ref, out_ref,
    near, table, dense_s, l_table, dense_l, total, send_sem, recv_sem,
):
    r, c, x, outer, skip, first_quad = place(row_count)
    k = c % 2
    up, down = r < row_count - 1, r > 0
    has_next = jnp.where(x == 0, up, down)
    has_prev = jnp.where(x == 0, down, up)
    next_row = jnp.where(x == 0, r + 1, r - 1)
    core = (r, 2 * x + 1 - k)
    across = (r, 2 * (1 - x) + k)
    ahead = (next_row, c)
    mine, theirs = c, 2 * (1 - x) + k
    low = lax.broadcasted_iota(jnp.int32, (B, 128), 1) < B

    def flip(t):
        return jnp.where(x == 1, t, 5 - t)

    def copy(src_chunk, dst_chunk, part, index, device):
        return pltpu.make_async_remote_copy(
            src_ref=near.at[src_chunk, part],
            dst_ref=near.at[dst_chunk, part],
            send_sem=send_sem.at[index],
            recv_sem=recv_sem.at[index],
            device_id=device,
            device_id_type=MESH,
        )

    def x_copy(s):
        return copy(jnp.where(x == 0, s + 2, 3 - s), jnp.where(x == 0, s, 5 - s), mine, X0 + s, across)

    def a_copy(s):
        return copy(flip(s), flip(s), mine, A0 + s, core)

    def c_copy(s):
        return copy(flip(s), flip(4 + s), mine, C0 + s, ahead)

    def e_copy(s):
        return copy(flip(s), flip(4 + s), theirs, E0 + s, ahead)

    def d_copy(s):
        return copy(flip(s), flip(s), theirs, D0 + s, core)

    def f_copy(s):
        return copy(flip(4 + s), flip(4 + s), mine, F0 + s, core)

    def g_copy(s):
        return copy(flip(4 + s), flip(4 + s), theirs, G0 + s, core)

    barrier = pltpu.get_barrier_semaphore()
    pl.semaphore_signal(barrier, inc=1, device_id=core, device_id_type=MESH)
    pl.semaphore_signal(barrier, inc=1, device_id=across, device_id_type=MESH)

    @pl.when(up)
    def _():
        pl.semaphore_signal(barrier, inc=1, device_id=(r + 1, c), device_id_type=MESH)

    @pl.when(down)
    def _():
        pl.semaphore_signal(barrier, inc=1, device_id=(r - 1, c), device_id_type=MESH)

    @pl.loop(0, 16)
    def _(pair):
        chunk = pair // 4 + 2 * (1 - x)
        at = lax.rem(pair, 4) * 5
        for odd in range(2):
            for t in range(2):
                near[chunk, mine, at + 2 * odd + t] = s_ref[2 * pair + odd, :, t * 128 : t * 128 + 128]
        near[chunk, mine, at + 4] = jnp.concatenate(
            [s_ref[2 * pair, :, 256:320], s_ref[2 * pair + 1, :, 256:320]], axis=1
        )

    pl.semaphore_wait(barrier, 2 + up.astype(jnp.int32) + down.astype(jnp.int32))

    for s in range(4):
        x_copy(s).start()
        if s < 2:

            @pl.when(has_next)
            def _():
                c_copy(s).start()

        a_copy(s).start()

    table[ZERO_S] = jnp.zeros((B, 128), jnp.bfloat16)
    l_table[30] = jnp.zeros((B, 128), jnp.bfloat16)

    @pl.loop(0, 8)
    def _(i):
        for t in range(15):
            v = l_ref[i, :, t * 128 : t * 128 + 128]
            l_table[t] = v
            l_table[15 + t] = swap(v)
        rows = pl.ds(pl.multiple_of(i * B, B), B)
        for quad in range(10):
            for half in range(2):
                at = quad * 4 + half * 2
                dense_l[quad, rows, half * 128 : half * 128 + 128] = jnp.where(
                    low, l_table[lt_ref[i, at]], l_table[lt_ref[i, at + 1]]
                )

    @pl.loop(0, 2 * QUADS + 1)
    def _(q):
        total[q] = jnp.zeros(total.shape[1:], jnp.float32)

    quad_count = 8 * row_count
    base_quad = jnp.clip(first_quad - 3, 0, quad_count - QUADS)

    def multiply(chunk):
        view = chunk - skip

        @pl.loop(0, PARTS)
        def _(p):
            for t in range(TILES):
                v = near[chunk, p, t]
                table[p * TILES + t] = v
                table[80 + p * TILES + t] = swap(v)

        @pl.loop(0, 2)
        def _(j):
            quad = view * 2 + j
            for row in range(4):
                for w in range(2 * SPAN):
                    dense_s[w // 2, row * B : row * B + B, (w % 2) * 128 : (w % 2) * 128 + 128] = jnp.where(
                        low,
                        table[t_ref[quad * 4 + row, 2 * w]],
                        table[t_ref[quad * 4 + row, 2 * w + 1]],
                    )
            start = 2 * (jnp.clip(first_quad + quad - 3, 0, quad_count - SPAN) - base_quad)
            for w in range(SPAN):
                part = jnp.dot(dense_l[quad], dense_s[w], preferred_element_type=jnp.float32)
                total[start + 2 * w] += part[:, :128]
                total[start + 2 * w + 1] += part[:, 128:]

    @pl.loop(0, 6)
    def _(e):
        for s, when in enumerate((0, 1, 3, 4)):

            @pl.when(e == when)
            def _():
                x_copy(s).wait_recv()
                d_copy(s).start()
                if s < 2:

                    @pl.when(has_next)
                    def _():
                        e_copy(s).start()

                a_copy(s).wait_recv()
                d_copy(s).wait_recv()

        for s, when in enumerate((2, 5)):

            @pl.when((e == when) & has_prev)
            def _():
                c_copy(s).wait_recv()
                f_copy(s).start()
                e_copy(s).wait_recv()
                g_copy(s).start()
                f_copy(s).wait_recv()
                g_copy(s).wait_recv()

        order = jnp.where(e < 2, e, jnp.where(e == 2, 4, jnp.where(e == 5, 5, e - 1)))

        @pl.when(jnp.where(outer, e >= 1, e <= 4))
        def _():
            multiply(flip(order))

    @pl.loop(0, 8)
    def _(i):
        rows = pl.ds(pl.multiple_of(i * B, B), B)
        for m in range(12):
            left, right = ct_ref[i, 2 * m], ct_ref[i, 2 * m + 1]
            a, b = total[left // 2, rows, :], total[right // 2, rows, :]
            a = jnp.where(left % 2 == 0, a, pltpu.roll(a, B, 1))
            b = jnp.where(right % 2 == 1, b, pltpu.roll(b, B, 1))
            out_ref[i, :, m * 128 : m * 128 + 128] = jnp.where(low, a, b).astype(jnp.bfloat16)

    for s in range(4):
        x_copy(s).wait_send()
        a_copy(s).wait_send()
        d_copy(s).wait_send()
    for s in range(2):

        @pl.when(has_next)
        def _():
            c_copy(s).wait_send()
            e_copy(s).wait_send()

        @pl.when(has_prev)
        def _():
            f_copy(s).wait_send()
            g_copy(s).wait_send()


def tables(row_count, l_index, s_cols, c_index):
    first_quad = place(row_count)[-1]
    quad_count = 8 * row_count
    rows = 4 * VIEW * 2
    row_ids = 4 * first_quad + lax.iota(jnp.int32, rows)
    near_cols = lax.dynamic_slice_in_dim(
        jnp.pad(s_cols, ((32, 32), (0, 0)), constant_values=-1), 4 * first_quad + 32, rows, axis=0
    )
    starts = 4 * jnp.clip(row_ids // 4 - 3, 0, quad_count - SPAN)
    at = lax.broadcasted_iota(jnp.int32, (rows, 4 * SPAN, PARTS * KSP), 0)
    col = lax.broadcasted_iota(jnp.int32, at.shape, 1)
    slot = lax.broadcasted_iota(jnp.int32, at.shape, 2)
    part, within = slot // KSP, slot % KSP
    odd = at % 2
    tile = jnp.where(within < 4, 2 * odd + within // 2, 4)
    half = jnp.where(within < 4, within % 2, odd)
    code = part * TILES + ((at // 2) % 4) * 5 + tile + 80 * (half != col % 2)
    hit = near_cols[:, None, :] == starts[:, None, None] + col
    s_table = ZERO_S + jnp.sum(jnp.where(hit, code - ZERO_S, 0), axis=2, dtype=jnp.int32)

    shape = (l_index.shape[0], rows, l_index.shape[1])
    at = lax.broadcasted_iota(jnp.int32, shape, 1)
    slot = lax.broadcasted_iota(jnp.int32, shape, 2)
    code = slot // 2 + 15 * (slot % 2 != at % 2)
    hit = l_index[:, None, :] == row_ids[None, :, None]
    l_table = 30 + jnp.sum(jnp.where(hit, code - 30, 0), axis=2, dtype=jnp.int32)

    spot = c_index - 4 * jnp.clip(first_quad - 3, 0, quad_count - QUADS)
    c_table = jnp.where((spot >= 0) & (spot < 4 * QUADS), spot, 4 * QUADS)
    return s_table, l_table, c_table


def shards(l_blocks, s_blocks, l_index, s_cols, c_index):
    row_count = lax.axis_size("rows")
    s_table, l_table, c_table = tables(row_count, l_index, s_cols, c_index)
    own = l_blocks.shape[0]
    vmem, smem = pl.BlockSpec(memory_space=pltpu.VMEM), pl.BlockSpec(memory_space=pltpu.SMEM)
    return pl.pallas_call(
        functools.partial(kernel, row_count),
        out_shape=jax.ShapeDtypeStruct((own, B, c_index.shape[1] * B), jnp.bfloat16),
        in_specs=[vmem, vmem, smem, smem, smem],
        out_specs=vmem,
        scratch_shapes=[
            pltpu.VMEM((CHUNKS, PARTS, TILES, B, 128), jnp.bfloat16),
            pltpu.VMEM((ZERO_S + 1, B, 128), jnp.bfloat16),
            pltpu.VMEM((SPAN, 4 * B, 4 * B), jnp.bfloat16),
            pltpu.VMEM((31, B, 128), jnp.bfloat16),
            pltpu.VMEM((2 * VIEW, own * B, 4 * B), jnp.bfloat16),
            pltpu.VMEM((2 * QUADS + 1, own * B, 128), jnp.float32),
            pltpu.SemaphoreType.DMA((20,)),
            pltpu.SemaphoreType.DMA((20,)),
        ],
        compiler_params=pltpu.CompilerParams(
            collective_id=0, has_side_effects=True, vmem_limit_bytes=56 * 1024 * 1024
        ),
        cost_estimate=pl.CostEstimate(flops=4_700_000_000, bytes_accessed=5_000_000, transcendentals=0),
    )(s_blocks, l_blocks, s_table, l_table, c_table)


def solution(mesh):
    return jax.shard_map(
        shards,
        mesh=mesh,
        in_specs=(
            P(("rows", "cols"), None, None),
            P("rows", None, "cols"),
            P(("rows", "cols"), None),
            P(),
            P(("rows", "cols"), None),
        ),
        out_specs=P(("rows", "cols"), None, None),
        check_vma=False,
    )
```

```python
import functools

import jax
import jax.numpy as jnp
from jax import lax
from jax.experimental import pallas as pl
from jax.experimental.pallas import tpu as pltpu
from jax.sharding import PartitionSpec as P

MESH = pl.DeviceIdType.MESH
B = 64
PARTS = 4
KSP = 5
SPAN = 8
TILES = 20
CHUNKS = 6
QUADS = 16
VIEW = 5
ZERO_S = 80
ZERO_L = 30
L_ROW, C_ROW = 40, 48
X0, A0, C0, E0, D0, F0, G0 = 0, 4, 8, 10, 12, 16, 18


def place(row_count):
    r = lax.axis_index("rows")
    c = lax.axis_index("cols")
    x = c // 2
    outer = jnp.where(x == 0, (c == 0) & (r > 0), (c == 3) & (r < row_count - 1))
    skip = jnp.where(x == 0, jnp.where(outer, 0, 1), jnp.where(outer, 1, 0))
    first_quad = 8 * r - 4 * (1 - x) + 2 * skip
    return r, c, x, outer, skip, first_quad


def swap(v):
    return jnp.concatenate([v[:, B:], v[:, :B]], axis=1)


def kernel(
    row_count, s_hbm, l_hbm, li_ref, sc_ref, ci_ref, out_hbm,
    s_ref, l_ref, out_ref, near, table, dense_s, l_table, dense_l, total, codes, spots,
    send_sem, recv_sem, in_sem, out_sem,
):
    r, c, x, outer, skip, first_quad = place(row_count)
    k = c % 2
    up, down = r < row_count - 1, r > 0
    has_next = jnp.where(x == 0, up, down)
    has_prev = jnp.where(x == 0, down, up)
    next_row = jnp.where(x == 0, r + 1, r - 1)
    core = (r, 2 * x + 1 - k)
    across = (r, 2 * (1 - x) + k)
    ahead = (next_row, c)
    mine, theirs = c, 2 * (1 - x) + k
    quad_count = 8 * row_count
    base_quad = jnp.clip(first_quad - 3, 0, quad_count - QUADS)

    barrier = pltpu.get_barrier_semaphore()
    pl.semaphore_signal(barrier, inc=1, device_id=core, device_id_type=MESH)
    pl.semaphore_signal(barrier, inc=1, device_id=across, device_id_type=MESH)

    @pl.when(up)
    def _():
        pl.semaphore_signal(barrier, inc=1, device_id=(r + 1, c), device_id_type=MESH)

    @pl.when(down)
    def _():
        pl.semaphore_signal(barrier, inc=1, device_id=(r - 1, c), device_id_type=MESH)

    s_in = pltpu.make_async_copy(s_hbm, s_ref, in_sem.at[0])
    l_in = pltpu.make_async_copy(l_hbm, l_ref, in_sem.at[1])
    s_in.start()
    l_in.start()

    low = lax.broadcasted_iota(jnp.int32, (B, 128), 1) < B

    def flip(t):
        return jnp.where(x == 1, t, 5 - t)

    def copy(src_chunk, dst_chunk, part, index, device):
        return pltpu.make_async_remote_copy(
            src_ref=near.at[src_chunk, part],
            dst_ref=near.at[dst_chunk, part],
            send_sem=send_sem.at[index],
            recv_sem=recv_sem.at[index],
            device_id=device,
            device_id_type=MESH,
        )

    def x_copy(s):
        return copy(jnp.where(x == 0, s + 2, 3 - s), jnp.where(x == 0, s, 5 - s), mine, X0 + s, across)

    def a_copy(s):
        return copy(flip(s), flip(s), mine, A0 + s, core)

    def c_copy(s):
        return copy(flip(s), flip(4 + s), mine, C0 + s, ahead)

    def e_copy(s):
        return copy(flip(s), flip(4 + s), theirs, E0 + s, ahead)

    def d_copy(s):
        return copy(flip(s), flip(s), theirs, D0 + s, core)

    def f_copy(s):
        return copy(flip(4 + s), flip(4 + s), mine, F0 + s, core)

    def g_copy(s):
        return copy(flip(4 + s), flip(4 + s), theirs, G0 + s, core)

    s_in.wait()

    @pl.loop(0, 16)
    def _(pair):
        chunk = pair // 4 + 2 * (1 - x)
        at = lax.rem(pair, 4) * 5
        for odd in range(2):
            for t in range(2):
                near[chunk, mine, at + 2 * odd + t] = s_ref[2 * pair + odd, :, t * 128 : t * 128 + 128]
        near[chunk, mine, at + 4] = jnp.concatenate(
            [s_ref[2 * pair, :, 256:320], s_ref[2 * pair + 1, :, 256:320]], axis=1
        )

    pl.semaphore_wait(barrier, 2 + up.astype(jnp.int32) + down.astype(jnp.int32))

    for s in range(4):
        x_copy(s).start()
        if s < 2:

            @pl.when(has_next)
            def _():
                c_copy(s).start()

        a_copy(s).start()

    row = lax.broadcasted_iota(jnp.int32, (8, 128), 0)
    lane = lax.broadcasted_iota(jnp.int32, (8, 128), 1)
    odd, side = row % 2, lane % 2
    for g in range(VIEW):
        first = 4 * first_quad + 8 * g
        inside = (first >= 0) & (first < 4 * quad_count)
        cols = sc_ref[pl.ds(pl.multiple_of(jnp.clip(first, 0, 4 * quad_count - 8), 8), 8), :]
        start = jnp.clip(first_quad + 2 * g - 3, 0, quad_count - SPAN)
        want = jnp.where(inside & (lane < 4 * SPAN), 4 * start + lane, -1)
        code = jnp.full((8, 128), ZERO_S, jnp.int32)
        for slot in range(PARTS * KSP):
            part, within = slot // KSP, slot % KSP
            tile = (part % 2) * TILES + (row // 2) * 5
            if within < 4:
                tile = tile + 2 * odd + within // 2 + jnp.where(side != within % 2, 40, 0)
            else:
                tile = tile + 4 + jnp.where(side != odd, 40, 0)
            code = jnp.where(cols[:, slot : slot + 1] == want, tile, code)
        codes[8 * g : 8 * g + 8, :] = code
    want = jnp.where(lane < 8 * VIEW, 4 * first_quad + lane, -1)
    code = jnp.full((8, 128), ZERO_L, jnp.int32)
    for slot in range(30):
        tile = slot // 2 + jnp.where(side != slot % 2, 15, 0)
        code = jnp.where(li_ref[:, slot : slot + 1] == want, tile, code)
    codes[L_ROW : L_ROW + 8, :] = code
    codes[C_ROW : C_ROW + 8, :] = jnp.zeros((8, 128), jnp.int32)
    spot = ci_ref[...] - 4 * base_quad
    codes[C_ROW : C_ROW + 8, 0 : spot.shape[1]] = jnp.where((spot >= 0) & (spot < 4 * QUADS), spot, 4 * QUADS)
    down_copy = pltpu.make_async_copy(codes, spots, in_sem.at[2])
    down_copy.start()

    @pl.loop(0, 2 * QUADS + 1)
    def _(q):
        total[q] = jnp.zeros(total.shape[1:], jnp.float32)

    table[ZERO_S] = jnp.zeros((B, 128), jnp.bfloat16)
    l_table[ZERO_L] = jnp.zeros((B, 128), jnp.bfloat16)
    down_copy.wait()
    l_in.wait()

    @pl.loop(0, 8)
    def _(i):
        for t in range(15):
            v = l_ref[i, :, t * 128 : t * 128 + 128]
            l_table[t] = v
            l_table[15 + t] = swap(v)
        rows = pl.ds(pl.multiple_of(i * B, B), B)
        for g in range(VIEW):
            for at in range(4):
                spot = 8 * g + 2 * at
                dense_l[g, rows, at * 128 : at * 128 + 128] = jnp.where(
                    low, l_table[spots[L_ROW + i, spot]], l_table[spots[L_ROW + i, spot + 1]]
                )

    def multiply(chunk, half):
        view = chunk - skip

        @pl.loop(0, 2)
        def _(p):
            for t in range(TILES):
                v = near[chunk, 2 * half + p, t]
                table[p * TILES + t] = v
                table[40 + p * TILES + t] = swap(v)

        start = jnp.clip(first_quad + 2 * view - 3, 0, quad_count - SPAN) - base_quad

        @pl.loop(0, 4)
        def _(n):
            for row in range(8):
                for w in range(2):
                    spot = 8 * n + 4 * w + 2 * half
                    dense_s[n, row * B : row * B + B, w * 128 : w * 128 + 128] = jnp.where(
                        low, table[spots[view * 8 + row, spot]], table[spots[view * 8 + row, spot + 1]]
                    )
            part = jnp.dot(dense_l[view], dense_s[n], preferred_element_type=jnp.float32)
            at = 2 * (start + 2 * n) + half
            total[at] += part[:, :128]
            total[at + 2] += part[:, 128:]

    events = ("A0", "A1", "A2", "A3", "X0", "C0", "X1", "C1", "E0", "X2", "X3", "E1")

    @pl.loop(0, len(events))
    def _(e):
        order = e * 0
        for index, (kind, s) in enumerate(events):
            s = int(s)
            order = jnp.where(e == index, s if kind in "AX" else 4 + s, order)

            @pl.when((e == index) & (has_prev if kind in "CE" else e >= 0))
            def _():
                if kind == "A":
                    a_copy(s).wait_recv()
                elif kind == "X":
                    x_copy(s).wait_recv()
                    d_copy(s).start()
                    if s < 2:

                        @pl.when(has_next)
                        def _():
                            e_copy(s).start()

                    d_copy(s).wait_recv()
                elif kind == "C":
                    c_copy(s).wait_recv()
                    f_copy(s).start()
                    f_copy(s).wait_recv()
                else:
                    e_copy(s).wait_recv()
                    g_copy(s).start()
                    g_copy(s).wait_recv()

        own_half = e * 0
        for index, (kind, s) in enumerate(events):
            own_half = jnp.where(e == index, 1 if kind in "AC" else 0, own_half)
        halo = order >= 4

        @pl.when(jnp.where(outer, order != 0, order != 5) & (has_prev | jnp.logical_not(halo)))
        def _():
            multiply(flip(order), jnp.where(own_half == 1, x, 1 - x))

    @pl.loop(0, 8)
    def _(i):
        rows = pl.ds(pl.multiple_of(i * B, B), B)
        for m in range(12):
            left, right = spots[C_ROW + i, 2 * m], spots[C_ROW + i, 2 * m + 1]
            a, b = total[left // 2, rows, :], total[right // 2, rows, :]
            straight = jnp.where(low, a, b)
            crossed = pltpu.roll(jnp.where(low, b, a), B, 1)
            keep = jnp.where(low, 1 - left % 2, right % 2) == 1
            out_ref[i, :, m * 128 : m * 128 + 128] = jnp.where(keep, straight, crossed).astype(jnp.bfloat16)
        pltpu.make_async_copy(out_ref.at[i], out_hbm.at[i], out_sem.at[i]).start()

    for s in range(4):
        x_copy(s).wait_send()
        a_copy(s).wait_send()
        d_copy(s).wait_send()
    for s in range(2):

        @pl.when(has_next)
        def _():
            c_copy(s).wait_send()
            e_copy(s).wait_send()

        @pl.when(has_prev)
        def _():
            f_copy(s).wait_send()
            g_copy(s).wait_send()

    @pl.loop(0, 8)
    def _(i):
        pltpu.make_async_copy(out_ref.at[i], out_hbm.at[i], out_sem.at[i]).wait()


def shards(l_blocks, s_blocks, l_index, s_cols, c_index):
    row_count = lax.axis_size("rows")
    own, kept = l_blocks.shape[0], c_index.shape[1]
    vmem, hbm = pl.BlockSpec(memory_space=pltpu.VMEM), pl.BlockSpec(memory_space=pl.ANY)
    return pl.pallas_call(
        functools.partial(kernel, row_count),
        out_shape=jax.ShapeDtypeStruct((own, B, kept * B), jnp.bfloat16),
        in_specs=[hbm, hbm, vmem, vmem, vmem],
        out_specs=hbm,
        scratch_shapes=[
            pltpu.VMEM(s_blocks.shape, jnp.bfloat16),
            pltpu.VMEM(l_blocks.shape, jnp.bfloat16),
            pltpu.VMEM((own, B, kept * B), jnp.bfloat16),
            pltpu.VMEM((CHUNKS, PARTS, TILES, B, 128), jnp.bfloat16),
            pltpu.VMEM((ZERO_S + 1, B, 128), jnp.bfloat16),
            pltpu.VMEM((4, 8 * B, 4 * B), jnp.bfloat16),
            pltpu.VMEM((ZERO_L + 1, B, 128), jnp.bfloat16),
            pltpu.VMEM((VIEW, own * B, 8 * B), jnp.bfloat16),
            pltpu.VMEM((2 * QUADS + 1, own * B, 128), jnp.float32),
            pltpu.VMEM((C_ROW + 8, 128), jnp.int32),
            pltpu.SMEM((C_ROW + 8, 128), jnp.int32),
            pltpu.SemaphoreType.DMA((20,)),
            pltpu.SemaphoreType.DMA((20,)),
            pltpu.SemaphoreType.DMA((3,)),
            pltpu.SemaphoreType.DMA((8,)),
        ],
        compiler_params=pltpu.CompilerParams(
            collective_id=0, has_side_effects=True, vmem_limit_bytes=56 * 1024 * 1024
        ),
        cost_estimate=pl.CostEstimate(flops=4_700_000_000, bytes_accessed=5_000_000, transcendentals=0),
    )(s_blocks, l_blocks, l_index, s_cols, c_index)


def solution(mesh):
    return jax.shard_map(
        shards,
        mesh=mesh,
        in_specs=(
            P(("rows", "cols"), None, None),
            P("rows", None, "cols"),
            P(("rows", "cols"), None),
            P(),
            P(("rows", "cols"), None),
        ),
        out_specs=P(("rows", "cols"), None, None),
        check_vma=False,
    )
```

```python
import functools

import jax
import jax.numpy as jnp
from jax import lax
from jax.experimental import pallas as pl
from jax.experimental.pallas import tpu as pltpu
from jax.sharding import PartitionSpec as P

MESH = pl.DeviceIdType.MESH
B = 64
PARTS = 4
KSP = 5
SPAN = 8
TILES = 20
CHUNKS = 6
QUADS = 16
VIEW = 5
ZERO_S = 80
ZERO_L = 30
L_ROW, C_ROW = 32, 40
X0, A0, C0, E0, D0, F0, G0 = 0, 4, 8, 10, 12, 16, 18


def place(row_count):
    r = lax.axis_index("rows")
    c = lax.axis_index("cols")
    x = c // 2
    outer = jnp.where(x == 0, (c == 0) & (r > 0), (c == 3) & (r < row_count - 1))
    skip = jnp.where(x == 0, jnp.where(outer, 0, 1), jnp.where(outer, 1, 0))
    first_quad = 8 * r - 4 * (1 - x) + 2 * skip
    return r, c, x, outer, skip, first_quad


def swap(v):
    return jnp.concatenate([v[:, B:], v[:, :B]], axis=1)


def kernel(
    row_count, s_hbm, l_hbm, li_ref, sc_ref, ci_ref, out_ref,
    s_ref, l_ref, near, table, dense_s, l_table, dense_l, total, codes, spots,
    send_sem, recv_sem, in_sem,
):
    r, c, x, outer, skip, first_quad = place(row_count)
    k = c % 2
    up, down = r < row_count - 1, r > 0
    has_next = jnp.where(x == 0, up, down)
    has_prev = jnp.where(x == 0, down, up)
    next_row = jnp.where(x == 0, r + 1, r - 1)
    core = (r, 2 * x + 1 - k)
    across = (r, 2 * (1 - x) + k)
    ahead = (next_row, c)
    mine, theirs = c, 2 * (1 - x) + k
    quad_count = 8 * row_count
    base_quad = jnp.clip(first_quad - 3, 0, quad_count - QUADS)

    barrier = pltpu.get_barrier_semaphore()
    pl.semaphore_signal(barrier, inc=1, device_id=core, device_id_type=MESH)
    pl.semaphore_signal(barrier, inc=1, device_id=across, device_id_type=MESH)

    @pl.when(up)
    def _():
        pl.semaphore_signal(barrier, inc=1, device_id=(r + 1, c), device_id_type=MESH)

    @pl.when(down)
    def _():
        pl.semaphore_signal(barrier, inc=1, device_id=(r - 1, c), device_id_type=MESH)

    s_in = pltpu.make_async_copy(s_hbm, s_ref, in_sem.at[0])
    l_in = pltpu.make_async_copy(l_hbm, l_ref, in_sem.at[1])
    s_in.start()
    l_in.start()

    low = lax.broadcasted_iota(jnp.int32, (B, 128), 1) < B

    def flip(t):
        return jnp.where(x == 1, t, 5 - t)

    def copy(src_chunk, dst_chunk, part, index, device):
        return pltpu.make_async_remote_copy(
            src_ref=near.at[src_chunk, part],
            dst_ref=near.at[dst_chunk, part],
            send_sem=send_sem.at[index],
            recv_sem=recv_sem.at[index],
            device_id=device,
            device_id_type=MESH,
        )

    def x_copy(s):
        return copy(jnp.where(x == 0, s + 2, 3 - s), jnp.where(x == 0, s, 5 - s), mine, X0 + s, across)

    def a_copy(s):
        return copy(flip(s), flip(s), mine, A0 + s, core)

    def c_copy(s):
        return copy(flip(s), flip(4 + s), mine, C0 + s, ahead)

    def e_copy(s):
        return copy(flip(s), flip(4 + s), theirs, E0 + s, ahead)

    def d_copy(s):
        return copy(flip(s), flip(s), theirs, D0 + s, core)

    def f_copy(s):
        return copy(flip(4 + s), flip(4 + s), mine, F0 + s, core)

    def g_copy(s):
        return copy(flip(4 + s), flip(4 + s), theirs, G0 + s, core)

    s_in.wait()

    @pl.loop(0, 16)
    def _(pair):
        chunk = pair // 4 + 2 * (1 - x)
        at = lax.rem(pair, 4) * 5
        for odd in range(2):
            for t in range(2):
                near[chunk, mine, at + 2 * odd + t] = s_ref[2 * pair + odd, :, t * 128 : t * 128 + 128]
        near[chunk, mine, at + 4] = jnp.concatenate(
            [s_ref[2 * pair, :, 256:320], s_ref[2 * pair + 1, :, 256:320]], axis=1
        )

    pl.semaphore_wait(barrier, 2 + up.astype(jnp.int32) + down.astype(jnp.int32))

    for s in range(4):
        x_copy(s).start()
        if s < 2:

            @pl.when(has_next)
            def _():
                c_copy(s).start()

        a_copy(s).start()

    base_row = 128 * jnp.clip(4 * first_quad // 128, 0, 4 * quad_count // 128 - 2)
    cols = sc_ref[:, pl.ds(pl.multiple_of(base_row, 128), 256)]
    want_at = lax.broadcasted_iota(jnp.int32, (4 * SPAN, 256), 0)
    row = lax.broadcasted_iota(jnp.int32, (4 * SPAN, 256), 1)
    odd, side = row % 2, want_at % 2
    want = 4 * jnp.clip(2 * ((base_row + row) // 8) - 3, 0, quad_count - SPAN) + want_at
    first_tile = ((row // 2) % 4) * 5
    code = jnp.full((4 * SPAN, 256), ZERO_S, jnp.int32)
    for within in range(KSP):
        if within < 4:
            tile = first_tile + 2 * odd + within // 2 + jnp.where(side != within % 2, 40, 0)
        else:
            tile = first_tile + 4 + jnp.where(side != odd, 40, 0)
        for part in range(PARTS):
            slot = part * KSP + within
            code = jnp.where(cols[slot : slot + 1, :] == want, tile + (part % 2) * TILES, code)
    codes[0 : 4 * SPAN, :] = code
    lane = lax.broadcasted_iota(jnp.int32, (8, 256), 1)
    side = lane % 2
    want = jnp.where(lane < 8 * VIEW, 4 * first_quad + lane, -1)
    code = jnp.full((8, 256), ZERO_L, jnp.int32)
    for slot in range(30):
        tile = slot // 2 + jnp.where(side != slot % 2, 15, 0)
        code = jnp.where(li_ref[:, slot : slot + 1] == want, tile, code)
    codes[L_ROW : L_ROW + 8, :] = code
    codes[C_ROW : C_ROW + 8, :] = jnp.zeros((8, 256), jnp.int32)
    spot = ci_ref[...] - 4 * base_quad
    codes[C_ROW : C_ROW + 8, 0 : spot.shape[1]] = jnp.where((spot >= 0) & (spot < 4 * QUADS), spot, 4 * QUADS)
    down_copy = pltpu.make_async_copy(codes, spots, in_sem.at[2])
    down_copy.start()

    @pl.loop(0, 2 * QUADS + 1)
    def _(q):
        total[q] = jnp.zeros(total.shape[1:], jnp.float32)

    table[ZERO_S] = jnp.zeros((B, 128), jnp.bfloat16)
    l_table[ZERO_L] = jnp.zeros((B, 128), jnp.bfloat16)
    down_copy.wait()
    l_in.wait()

    @pl.loop(0, 8)
    def _(i):
        for t in range(15):
            v = l_ref[i, :, t * 128 : t * 128 + 128]
            l_table[t] = v
            l_table[15 + t] = swap(v)
        rows = pl.ds(pl.multiple_of(i * B, B), B)
        for g in range(VIEW):
            for at in range(4):
                spot = 8 * g + 2 * at
                dense_l[g, rows, at * 128 : at * 128 + 128] = jnp.where(
                    low, l_table[spots[L_ROW + i, spot]], l_table[spots[L_ROW + i, spot + 1]]
                )

    def multiply(chunk, half):
        view = chunk - skip

        @pl.loop(0, 2)
        def _(p):
            for t in range(TILES):
                v = near[chunk, 2 * half + p, t]
                table[p * TILES + t] = v
                table[40 + p * TILES + t] = swap(v)

        start = jnp.clip(first_quad + 2 * view - 3, 0, quad_count - SPAN) - base_quad
        first = 4 * first_quad - base_row + view * 8

        @pl.loop(0, 4)
        def _(n):
            for row in range(8):
                for w in range(2):
                    spot = 8 * n + 4 * w + 2 * half
                    dense_s[n, row * B : row * B + B, w * 128 : w * 128 + 128] = jnp.where(
                        low, table[spots[spot, first + row]], table[spots[spot + 1, first + row]]
                    )
            part = jnp.dot(dense_l[view], dense_s[n], preferred_element_type=jnp.float32)
            at = 2 * (start + 2 * n) + half
            total[at] += part[:, :128]
            total[at + 2] += part[:, 128:]

    events = ("A0", "A1", "A2", "A3", "X0", "C0", "X1", "C1", "E0", "X2", "X3", "E1")

    @pl.loop(0, len(events))
    def _(e):
        order = e * 0
        for index, (kind, s) in enumerate(events):
            s = int(s)
            order = jnp.where(e == index, s if kind in "AX" else 4 + s, order)

            @pl.when((e == index) & (has_prev if kind in "CE" else e >= 0))
            def _():
                if kind == "A":
                    a_copy(s).wait_recv()
                elif kind == "X":
                    x_copy(s).wait_recv()
                    d_copy(s).start()
                    if s < 2:

                        @pl.when(has_next)
                        def _():
                            e_copy(s).start()

                    d_copy(s).wait_recv()
                elif kind == "C":
                    c_copy(s).wait_recv()
                    f_copy(s).start()
                    f_copy(s).wait_recv()
                else:
                    e_copy(s).wait_recv()
                    g_copy(s).start()
                    g_copy(s).wait_recv()

        own_half = e * 0
        for index, (kind, s) in enumerate(events):
            own_half = jnp.where(e == index, 1 if kind in "AC" else 0, own_half)
        halo = order >= 4

        @pl.when(jnp.where(outer, order != 0, order != 5) & (has_prev | jnp.logical_not(halo)))
        def _():
            multiply(flip(order), jnp.where(own_half == 1, x, 1 - x))

    @pl.loop(0, 8)
    def _(i):
        rows = pl.ds(pl.multiple_of(i * B, B), B)
        for m in range(12):
            left, right = spots[C_ROW + i, 2 * m], spots[C_ROW + i, 2 * m + 1]
            a, b = total[left // 2, rows, :], total[right // 2, rows, :]
            straight = jnp.where(low, a, b)
            crossed = pltpu.roll(jnp.where(low, b, a), B, 1)
            keep = jnp.where(low, 1 - left % 2, right % 2) == 1
            out_ref[i, :, m * 128 : m * 128 + 128] = jnp.where(keep, straight, crossed).astype(jnp.bfloat16)

    for s in range(4):
        x_copy(s).wait_send()
        a_copy(s).wait_send()
        d_copy(s).wait_send()
    for s in range(2):

        @pl.when(has_next)
        def _():
            c_copy(s).wait_send()
            e_copy(s).wait_send()

        @pl.when(has_prev)
        def _():
            f_copy(s).wait_send()
            g_copy(s).wait_send()


def shards(l_blocks, s_blocks, l_index, s_cols, c_index):
    row_count = lax.axis_size("rows")
    own, kept = l_blocks.shape[0], c_index.shape[1]
    vmem, hbm = pl.BlockSpec(memory_space=pltpu.VMEM), pl.BlockSpec(memory_space=pl.ANY)
    return pl.pallas_call(
        functools.partial(kernel, row_count),
        out_shape=pltpu.VMEM((own, B, kept * B), jnp.bfloat16),
        in_specs=[hbm, hbm, vmem, vmem, vmem],
        out_specs=vmem,
        scratch_shapes=[
            pltpu.VMEM(s_blocks.shape, jnp.bfloat16),
            pltpu.VMEM(l_blocks.shape, jnp.bfloat16),
            pltpu.VMEM((CHUNKS, PARTS, TILES, B, 128), jnp.bfloat16),
            pltpu.VMEM((ZERO_S + 1, B, 128), jnp.bfloat16),
            pltpu.VMEM((4, 8 * B, 4 * B), jnp.bfloat16),
            pltpu.VMEM((ZERO_L + 1, B, 128), jnp.bfloat16),
            pltpu.VMEM((VIEW, own * B, 8 * B), jnp.bfloat16),
            pltpu.VMEM((2 * QUADS + 1, own * B, 128), jnp.float32),
            pltpu.VMEM((C_ROW + 8, 256), jnp.int32),
            pltpu.SMEM((C_ROW + 8, 256), jnp.int32),
            pltpu.SemaphoreType.DMA((20,)),
            pltpu.SemaphoreType.DMA((20,)),
            pltpu.SemaphoreType.DMA((3,)),
        ],
        compiler_params=pltpu.CompilerParams(
            collective_id=0, has_side_effects=True, vmem_limit_bytes=56 * 1024 * 1024
        ),
        cost_estimate=pl.CostEstimate(flops=4_700_000_000, bytes_accessed=5_000_000, transcendentals=0),
    )(s_blocks, l_blocks, l_index, s_cols.T, c_index)


def solution(mesh):
    return jax.shard_map(
        shards,
        mesh=mesh,
        in_specs=(
            P(("rows", "cols"), None, None),
            P("rows", None, "cols"),
            P(("rows", "cols"), None),
            P(),
            P(("rows", "cols"), None),
        ),
        out_specs=P(("rows", "cols"), None, None),
        check_vma=False,
    )
```

```python
import functools

import jax
import jax.numpy as jnp
from jax import lax
from jax.experimental import pallas as pl
from jax.experimental.pallas import tpu as pltpu
from jax.sharding import PartitionSpec as P

MESH = pl.DeviceIdType.MESH
B = 64
PARTS = 4
KSP = 5
SPAN = 8
TILES = 20
CHUNKS = 6
QUADS = 16
VIEW = 5
ZERO_S = 80
ZERO_L = 30
L_ROW, C_ROW = 32, 40
X0, A0, C0, E0, D0, F0, G0 = 0, 4, 8, 10, 12, 16, 18


def place(row_count):
    r = lax.axis_index("rows")
    c = lax.axis_index("cols")
    x = c // 2
    outer = jnp.where(x == 0, (c == 0) & (r > 0), (c == 3) & (r < row_count - 1))
    skip = jnp.where(x == 0, jnp.where(outer, 0, 1), jnp.where(outer, 1, 0))
    first_quad = 8 * r - 4 * (1 - x) + 2 * skip
    return r, c, x, outer, skip, first_quad


def swap(v):
    return jnp.concatenate([v[:, B:], v[:, :B]], axis=1)


def kernel(
    row_count, s_hbm, l_hbm, li_ref, sc_ref, ci_ref, out_ref,
    s_ref, l_ref, near, table, dense_s, l_table, dense_l, total, codes, spots,
    send_sem, recv_sem, in_sem,
):
    r, c, x, outer, skip, first_quad = place(row_count)
    k = c % 2
    up, down = r < row_count - 1, r > 0
    has_next = jnp.where(x == 0, up, down)
    has_prev = jnp.where(x == 0, down, up)
    next_row = jnp.where(x == 0, r + 1, r - 1)
    core = (r, 2 * x + 1 - k)
    across = (r, 2 * (1 - x) + k)
    ahead = (next_row, c)
    mine, theirs = c, 2 * (1 - x) + k
    quad_count = 8 * row_count
    base_quad = jnp.clip(first_quad - 3, 0, quad_count - QUADS)

    barrier = pltpu.get_barrier_semaphore()
    pl.semaphore_signal(barrier, inc=1, device_id=core, device_id_type=MESH)
    pl.semaphore_signal(barrier, inc=1, device_id=across, device_id_type=MESH)

    @pl.when(up)
    def _():
        pl.semaphore_signal(barrier, inc=1, device_id=(r + 1, c), device_id_type=MESH)

    @pl.when(down)
    def _():
        pl.semaphore_signal(barrier, inc=1, device_id=(r - 1, c), device_id_type=MESH)

    s_in = pltpu.make_async_copy(s_hbm, s_ref, in_sem.at[0])
    l_in = pltpu.make_async_copy(l_hbm, l_ref, in_sem.at[1])
    s_in.start()
    l_in.start()

    low = lax.broadcasted_iota(jnp.int32, (B, 128), 1) < B

    def flip(t):
        return jnp.where(x == 1, t, 5 - t)

    def copy(src_chunk, dst_chunk, part, index, device):
        return pltpu.make_async_remote_copy(
            src_ref=near.at[src_chunk, part],
            dst_ref=near.at[dst_chunk, part],
            send_sem=send_sem.at[index],
            recv_sem=recv_sem.at[index],
            device_id=device,
            device_id_type=MESH,
        )

    def x_copy(s):
        return copy(jnp.where(x == 0, s + 2, 3 - s), jnp.where(x == 0, s, 5 - s), mine, X0 + s, across)

    def a_copy(s):
        return copy(flip(s), flip(s), mine, A0 + s, core)

    def c_copy(s):
        return copy(flip(s), flip(4 + s), mine, C0 + s, ahead)

    def e_copy(s):
        return copy(flip(s), flip(4 + s), theirs, E0 + s, ahead)

    def d_copy(s):
        return copy(flip(s), flip(s), theirs, D0 + s, core)

    def f_copy(s):
        return copy(flip(4 + s), flip(4 + s), mine, F0 + s, core)

    def g_copy(s):
        return copy(flip(4 + s), flip(4 + s), theirs, G0 + s, core)

    s_in.wait()

    for step in (0, 3, 1, 2):
        group_chunk = jnp.where(x == 0, step, 3 - step)
        chunk = group_chunk + 2 * (1 - x)

        @pl.loop(0, 4)
        def _(pair):
            at = pair * 5
            source = 8 * group_chunk + 2 * pair
            for odd in range(2):
                for t in range(2):
                    near[chunk, mine, at + 2 * odd + t] = s_ref[source + odd, :, t * 128 : t * 128 + 128]
            near[chunk, mine, at + 4] = jnp.concatenate(
                [s_ref[source, :, 256:320], s_ref[source + 1, :, 256:320]], axis=1
            )

        if step == 0:
            pl.semaphore_wait(barrier, 2 + up.astype(jnp.int32) + down.astype(jnp.int32))
        if step < 2:
            x_copy(step).start()
        else:

            @pl.when(has_next)
            def _():
                c_copy(3 - step).start()

        a_copy(3 - step).start()

    base_row = 128 * jnp.clip(4 * first_quad // 128, 0, 4 * quad_count // 128 - 2)
    cols = sc_ref[:, pl.ds(pl.multiple_of(base_row, 128), 256)]
    want_at = lax.broadcasted_iota(jnp.int32, (4 * SPAN, 256), 0)
    row = lax.broadcasted_iota(jnp.int32, (4 * SPAN, 256), 1)
    odd, side = row % 2, want_at % 2
    want = 4 * jnp.clip(2 * ((base_row + row) // 8) - 3, 0, quad_count - SPAN) + want_at
    first_tile = ((row // 2) % 4) * 5
    code = jnp.full((4 * SPAN, 256), ZERO_S, jnp.int32)
    for within in range(KSP):
        if within < 4:
            tile = first_tile + 2 * odd + within // 2 + jnp.where(side != within % 2, 40, 0)
        else:
            tile = first_tile + 4 + jnp.where(side != odd, 40, 0)
        for part in range(PARTS):
            slot = part * KSP + within
            code = jnp.where(cols[slot : slot + 1, :] == want, tile + (part % 2) * TILES, code)
    codes[0 : 4 * SPAN, :] = code
    lane = lax.broadcasted_iota(jnp.int32, (8, 256), 1)
    side = lane % 2
    want = jnp.where(lane < 8 * VIEW, 4 * first_quad + lane, -1)
    code = jnp.full((8, 256), ZERO_L, jnp.int32)
    for slot in range(30):
        tile = slot // 2 + jnp.where(side != slot % 2, 15, 0)
        code = jnp.where(li_ref[:, slot : slot + 1] == want, tile, code)
    codes[L_ROW : L_ROW + 8, :] = code
    codes[C_ROW : C_ROW + 8, :] = jnp.zeros((8, 256), jnp.int32)
    spot = ci_ref[...] - 4 * base_quad
    codes[C_ROW : C_ROW + 8, 0 : spot.shape[1]] = jnp.where((spot >= 0) & (spot < 4 * QUADS), spot, 4 * QUADS)
    down_copy = pltpu.make_async_copy(codes, spots, in_sem.at[2])
    down_copy.start()

    @pl.loop(0, 2 * QUADS + 1)
    def _(q):
        total[q] = jnp.zeros(total.shape[1:], jnp.float32)

    table[ZERO_S] = jnp.zeros((B, 128), jnp.bfloat16)
    l_table[ZERO_L] = jnp.zeros((B, 128), jnp.bfloat16)
    down_copy.wait()
    l_in.wait()

    @pl.loop(0, 8)
    def _(i):
        for t in range(15):
            v = l_ref[i, :, t * 128 : t * 128 + 128]
            l_table[t] = v
            l_table[15 + t] = swap(v)
        rows = pl.ds(pl.multiple_of(i * B, B), B)
        for g in range(VIEW):
            for at in range(4):
                spot = 8 * g + 2 * at
                dense_l[g, rows, at * 128 : at * 128 + 128] = jnp.where(
                    low, l_table[spots[L_ROW + i, spot]], l_table[spots[L_ROW + i, spot + 1]]
                )

    def multiply(chunk, half):
        view = chunk - skip

        @pl.loop(0, 2)
        def _(p):
            for t in range(TILES):
                v = near[chunk, 2 * half + p, t]
                table[p * TILES + t] = v
                table[40 + p * TILES + t] = swap(v)

        start = jnp.clip(first_quad + 2 * view - 3, 0, quad_count - SPAN) - base_quad
        first = 4 * first_quad - base_row + view * 8

        @pl.loop(0, 4)
        def _(n):
            for row in range(8):
                for w in range(2):
                    spot = 8 * n + 4 * w + 2 * half
                    dense_s[n, row * B : row * B + B, w * 128 : w * 128 + 128] = jnp.where(
                        low, table[spots[spot, first + row]], table[spots[spot + 1, first + row]]
                    )
            part = jnp.dot(dense_l[view], dense_s[n], preferred_element_type=jnp.float32)
            at = 2 * (start + 2 * n) + half
            total[at] += part[:, :128]
            total[at + 2] += part[:, 128:]

    events = ("A0", "A1", "A2", "A3", "X0", "C0", "X1", "C1", "E0", "X2", "X3", "E1")

    @pl.loop(0, len(events))
    def _(e):
        order = e * 0
        for index, (kind, s) in enumerate(events):
            s = int(s)
            order = jnp.where(e == index, s if kind in "AX" else 4 + s, order)

            @pl.when((e == index) & (has_prev if kind in "CE" else e >= 0))
            def _():
                if kind == "A":
                    a_copy(s).wait_recv()
                elif kind == "X":
                    x_copy(s).wait_recv()
                    if s < 2:

                        @pl.when(has_next)
                        def _():
                            e_copy(s).start()

                        x_copy(s + 2).start()
                    d_copy(s).start()
                    d_copy(s).wait_recv()
                elif kind == "C":
                    c_copy(s).wait_recv()
                    f_copy(s).start()
                    f_copy(s).wait_recv()
                else:
                    e_copy(s).wait_recv()
                    g_copy(s).start()
                    g_copy(s).wait_recv()

        own_half = e * 0
        for index, (kind, s) in enumerate(events):
            own_half = jnp.where(e == index, 1 if kind in "AC" else 0, own_half)
        halo = order >= 4

        @pl.when(jnp.where(outer, order != 0, order != 5) & (has_prev | jnp.logical_not(halo)))
        def _():
            multiply(flip(order), jnp.where(own_half == 1, x, 1 - x))

    @pl.loop(0, 8)
    def _(i):
        rows = pl.ds(pl.multiple_of(i * B, B), B)
        for m in range(12):
            left, right = spots[C_ROW + i, 2 * m], spots[C_ROW + i, 2 * m + 1]
            a, b = total[left // 2, rows, :], total[right // 2, rows, :]
            straight = jnp.where(low, a, b)
            crossed = pltpu.roll(jnp.where(low, b, a), B, 1)
            keep = jnp.where(low, 1 - left % 2, right % 2) == 1
            out_ref[i, :, m * 128 : m * 128 + 128] = jnp.where(keep, straight, crossed).astype(jnp.bfloat16)

    for s in range(4):
        x_copy(s).wait_send()
        a_copy(s).wait_send()
        d_copy(s).wait_send()
    for s in range(2):

        @pl.when(has_next)
        def _():
            c_copy(s).wait_send()
            e_copy(s).wait_send()

        @pl.when(has_prev)
        def _():
            f_copy(s).wait_send()
            g_copy(s).wait_send()


def shards(l_blocks, s_blocks, l_index, s_cols, c_index):
    row_count = lax.axis_size("rows")
    own, kept = l_blocks.shape[0], c_index.shape[1]
    vmem, hbm = pl.BlockSpec(memory_space=pltpu.VMEM), pl.BlockSpec(memory_space=pl.ANY)
    return pl.pallas_call(
        functools.partial(kernel, row_count),
        out_shape=pltpu.VMEM((own, B, kept * B), jnp.bfloat16),
        in_specs=[hbm, hbm, vmem, vmem, vmem],
        out_specs=vmem,
        scratch_shapes=[
            pltpu.VMEM(s_blocks.shape, jnp.bfloat16),
            pltpu.VMEM(l_blocks.shape, jnp.bfloat16),
            pltpu.VMEM((CHUNKS, PARTS, TILES, B, 128), jnp.bfloat16),
            pltpu.VMEM((ZERO_S + 1, B, 128), jnp.bfloat16),
            pltpu.VMEM((4, 8 * B, 4 * B), jnp.bfloat16),
            pltpu.VMEM((ZERO_L + 1, B, 128), jnp.bfloat16),
            pltpu.VMEM((VIEW, own * B, 8 * B), jnp.bfloat16),
            pltpu.VMEM((2 * QUADS + 1, own * B, 128), jnp.float32),
            pltpu.VMEM((C_ROW + 8, 256), jnp.int32),
            pltpu.SMEM((C_ROW + 8, 256), jnp.int32),
            pltpu.SemaphoreType.DMA((20,)),
            pltpu.SemaphoreType.DMA((20,)),
            pltpu.SemaphoreType.DMA((3,)),
        ],
        compiler_params=pltpu.CompilerParams(
            collective_id=0, has_side_effects=True, vmem_limit_bytes=56 * 1024 * 1024
        ),
        cost_estimate=pl.CostEstimate(flops=4_700_000_000, bytes_accessed=5_000_000, transcendentals=0),
    )(s_blocks, l_blocks, l_index, s_cols.T, c_index)


def solution(mesh):
    return jax.shard_map(
        shards,
        mesh=mesh,
        in_specs=(
            P(("rows", "cols"), None, None),
            P("rows", None, "cols"),
            P(("rows", "cols"), None),
            P(),
            P(("rows", "cols"), None),
        ),
        out_specs=P(("rows", "cols"), None, None),
        check_vma=False,
    )
```

```python
import functools

import jax
import jax.numpy as jnp
from jax import lax
from jax.experimental import pallas as pl
from jax.experimental.pallas import tpu as pltpu
from jax.sharding import PartitionSpec as P

MESH = pl.DeviceIdType.MESH
B = 64
PARTS = 4
KSP = 5
SPAN = 8
TILES = 20
CHUNKS = 6
QUADS = 16
VIEW = 5
ZERO_S = 80
ZERO_L = 30
L_ROW, C_ROW = 32, 40
X0, A0, C0, E0, D0, F0, G0 = 0, 4, 8, 10, 12, 16, 18


def place(row_count):
    r = lax.axis_index("rows")
    c = lax.axis_index("cols")
    x = c // 2
    outer = jnp.where(x == 0, (c == 0) & (r > 0), (c == 3) & (r < row_count - 1))
    skip = jnp.where(x == 0, jnp.where(outer, 0, 1), jnp.where(outer, 1, 0))
    first_quad = 8 * r - 4 * (1 - x) + 2 * skip
    return r, c, x, outer, skip, first_quad


def swap(v):
    return jnp.concatenate([v[:, B:], v[:, :B]], axis=1)


def kernel(
    row_count, s_hbm, l_hbm, li_ref, sc_ref, ci_ref, out_ref,
    s_ref, l_ref, near, table, dense_s, l_table, dense_l, total, codes, spots,
    send_sem, recv_sem, in_sem,
):
    r, c, x, outer, skip, first_quad = place(row_count)
    k = c % 2
    up, down = r < row_count - 1, r > 0
    has_next = jnp.where(x == 0, up, down)
    has_prev = jnp.where(x == 0, down, up)
    next_row = jnp.where(x == 0, r + 1, r - 1)
    core = (r, 2 * x + 1 - k)
    across = (r, 2 * (1 - x) + k)
    ahead = (next_row, c)
    mine, theirs = c, 2 * (1 - x) + k
    quad_count = 8 * row_count
    base_quad = jnp.clip(first_quad - 3, 0, quad_count - QUADS)

    barrier = pltpu.get_barrier_semaphore()
    pl.semaphore_signal(barrier, inc=1, device_id=core, device_id_type=MESH)
    pl.semaphore_signal(barrier, inc=1, device_id=across, device_id_type=MESH)

    @pl.when(up)
    def _():
        pl.semaphore_signal(barrier, inc=1, device_id=(r + 1, c), device_id_type=MESH)

    @pl.when(down)
    def _():
        pl.semaphore_signal(barrier, inc=1, device_id=(r - 1, c), device_id_type=MESH)

    s_in = pltpu.make_async_copy(s_hbm, s_ref, in_sem.at[0])
    l_in = pltpu.make_async_copy(l_hbm, l_ref, in_sem.at[1])
    s_in.start()
    l_in.start()

    low = lax.broadcasted_iota(jnp.int32, (B, 128), 1) < B
    low16 = lax.broadcasted_iota(jnp.int16, (B, 128), 1) < B

    def flip(t):
        return jnp.where(x == 1, t, 5 - t)

    def copy(src_chunk, dst_chunk, part, index, device):
        return pltpu.make_async_remote_copy(
            src_ref=near.at[src_chunk, part],
            dst_ref=near.at[dst_chunk, part],
            send_sem=send_sem.at[index],
            recv_sem=recv_sem.at[index],
            device_id=device,
            device_id_type=MESH,
        )

    def x_copy(s):
        return copy(jnp.where(x == 0, s + 2, 3 - s), jnp.where(x == 0, s, 5 - s), mine, X0 + s, across)

    def a_copy(s):
        return copy(flip(s), flip(s), mine, A0 + s, core)

    def c_copy(s):
        return copy(flip(s), flip(4 + s), mine, C0 + s, ahead)

    def e_copy(s):
        return copy(flip(s), flip(4 + s), theirs, E0 + s, ahead)

    def d_copy(s):
        return copy(flip(s), flip(s), theirs, D0 + s, core)

    def f_copy(s):
        return copy(flip(4 + s), flip(4 + s), mine, F0 + s, core)

    def g_copy(s):
        return copy(flip(4 + s), flip(4 + s), theirs, G0 + s, core)

    s_in.wait()

    for step in (0, 3, 1, 2):
        group_chunk = jnp.where(x == 0, step, 3 - step)
        chunk = group_chunk + 2 * (1 - x)

        @pl.loop(0, 4)
        def _(pair):
            at = pair * 5
            source = 8 * group_chunk + 2 * pair
            for odd in range(2):
                for t in range(2):
                    near[chunk, mine, at + 2 * odd + t] = s_ref[source + odd, :, t * 128 : t * 128 + 128]
            near[chunk, mine, at + 4] = jnp.concatenate(
                [s_ref[source, :, 256:320], s_ref[source + 1, :, 256:320]], axis=1
            )

        if step == 0:
            pl.semaphore_wait(barrier, 2 + up.astype(jnp.int32) + down.astype(jnp.int32))
        if step < 2:
            x_copy(step).start()
        else:

            @pl.when(has_next)
            def _():
                c_copy(3 - step).start()

        a_copy(3 - step).start()

    base_row = 128 * jnp.clip(4 * first_quad // 128, 0, 4 * quad_count // 128 - 2)
    cols = sc_ref[:, pl.ds(pl.multiple_of(base_row, 128), 256)]
    want_at = lax.broadcasted_iota(jnp.int32, (4 * SPAN, 256), 0)
    row = lax.broadcasted_iota(jnp.int32, (4 * SPAN, 256), 1)
    odd, side = row % 2, want_at % 2
    want = 4 * jnp.clip(2 * ((base_row + row) // 8) - 3, 0, quad_count - SPAN) + want_at
    first_tile = ((row // 2) % 4) * 5
    code = jnp.full((4 * SPAN, 256), ZERO_S, jnp.int32)
    for within in range(KSP):
        if within < 4:
            tile = first_tile + 2 * odd + within // 2 + jnp.where(side != within % 2, 40, 0)
        else:
            tile = first_tile + 4 + jnp.where(side != odd, 40, 0)
        for part in range(PARTS):
            slot = part * KSP + within
            code = jnp.where(cols[slot : slot + 1, :] == want, tile + (part % 2) * TILES, code)
    codes[0 : 4 * SPAN, :] = code
    lane = lax.broadcasted_iota(jnp.int32, (8, 256), 1)
    side = lane % 2
    want = jnp.where(lane < 8 * VIEW, 4 * first_quad + lane, -1)
    code = jnp.full((8, 256), ZERO_L, jnp.int32)
    for slot in range(30):
        tile = slot // 2 + jnp.where(side != slot % 2, 15, 0)
        code = jnp.where(li_ref[:, slot : slot + 1] == want, tile, code)
    codes[L_ROW : L_ROW + 8, :] = code
    codes[C_ROW : C_ROW + 8, :] = jnp.zeros((8, 256), jnp.int32)
    spot = ci_ref[...] - 4 * base_quad
    codes[C_ROW : C_ROW + 8, 0 : spot.shape[1]] = jnp.where((spot >= 0) & (spot < 4 * QUADS), spot, 4 * QUADS)
    down_copy = pltpu.make_async_copy(codes, spots, in_sem.at[2])
    down_copy.start()

    @pl.loop(0, 2 * QUADS + 1)
    def _(q):
        total[q] = jnp.zeros(total.shape[1:], jnp.float32)

    table[ZERO_S] = jnp.zeros((B, 128), jnp.bfloat16)
    l_table[ZERO_L] = jnp.zeros((B, 128), jnp.bfloat16)
    down_copy.wait()
    l_in.wait()

    @pl.loop(0, 8)
    def _(i):
        for t in range(15):
            v = l_ref[i, :, t * 128 : t * 128 + 128]
            l_table[t] = v
            l_table[15 + t] = swap(v)
        rows = pl.ds(pl.multiple_of(i * B, B), B)
        for g in range(VIEW):
            for at in range(4):
                spot = 8 * g + 2 * at
                dense_l[g, rows, at * 128 : at * 128 + 128] = jnp.where(
                    low16, l_table[spots[L_ROW + i, spot]], l_table[spots[L_ROW + i, spot + 1]]
                )

    def multiply(chunk, half):
        view = chunk - skip

        @pl.loop(0, 2)
        def _(p):
            for t in range(TILES):
                v = near[chunk, 2 * half + p, t]
                table[p * TILES + t] = v
                table[40 + p * TILES + t] = swap(v)

        start = jnp.clip(first_quad + 2 * view - 3, 0, quad_count - SPAN) - base_quad
        first = 4 * first_quad - base_row + view * 8

        for n in range(4):
            for row in range(8):
                for w in range(2):
                    spot = 8 * n + 4 * w + 2 * half
                    dense_s[n, row * B : row * B + B, w * 128 : w * 128 + 128] = jnp.where(
                        low16, table[spots[spot, first + row]], table[spots[spot + 1, first + row]]
                    )
            part = jnp.dot(dense_l[view], dense_s[n], preferred_element_type=jnp.float32)
            at = 2 * (start + 2 * n) + half
            total[at] += part[:, :128]
            total[at + 2] += part[:, 128:]

    events = ("A0", "A1", "X0", "C0", "A2", "X1", "C1", "A3", "E0", "X2", "X3", "E1")

    def when_prev(action):
        pl.when(has_prev)(action)

    def arrive_x(s):
        x_copy(s).wait_recv()
        if s < 2:
            pl.when(has_next)(lambda: e_copy(s).start())
            x_copy(s + 2).start()
        d_copy(s).start()

    def arrive_c(s):
        c_copy(s).wait_recv()
        f_copy(s).start()

    def arrive_e(s):
        e_copy(s).wait_recv()
        g_copy(s).start()

    def before(kind, s):
        if kind == "A":
            a_copy(s).wait_recv()
        elif kind == "X":
            if s != 2:
                arrive_x(s)
                when_prev(lambda: arrive_e(1) if s == 3 else arrive_c(s))
            d_copy(s).wait_recv()
        elif kind == "C":
            when_prev(lambda: f_copy(s).wait_recv())
        else:
            if s == 0:
                when_prev(lambda: arrive_e(0))
                arrive_x(2)
            when_prev(lambda: g_copy(s).wait_recv())

    @pl.loop(0, len(events))
    def _(e):
        order = e * 0
        for index, (kind, s) in enumerate(events):
            order = jnp.where(e == index, int(s) if kind in "AX" else 4 + int(s), order)
            pl.when(e == index)(functools.partial(before, kind, int(s)))

        own_half = e * 0
        for index, (kind, s) in enumerate(events):
            own_half = jnp.where(e == index, 1 if kind in "AC" else 0, own_half)
        halo = order >= 4

        @pl.when(jnp.where(outer, order != 0, order != 5) & (has_prev | jnp.logical_not(halo)))
        def _():
            multiply(flip(order), jnp.where(own_half == 1, x, 1 - x))

    @pl.loop(0, 8)
    def _(i):
        rows = pl.ds(pl.multiple_of(i * B, B), B)
        for m in range(12):
            left, right = spots[C_ROW + i, 2 * m], spots[C_ROW + i, 2 * m + 1]
            a, b = total[left // 2, rows, :], total[right // 2, rows, :]
            straight = jnp.where(low, a, b)
            crossed = pltpu.roll(jnp.where(low, b, a), B, 1)
            keep = jnp.where(low, 1 - left % 2, right % 2) == 1
            out_ref[i, :, m * 128 : m * 128 + 128] = jnp.where(keep, straight, crossed).astype(jnp.bfloat16)

    for s in range(4):
        x_copy(s).wait_send()
        a_copy(s).wait_send()
        d_copy(s).wait_send()
    for s in range(2):

        @pl.when(has_next)
        def _():
            c_copy(s).wait_send()
            e_copy(s).wait_send()

        @pl.when(has_prev)
        def _():
            f_copy(s).wait_send()
            g_copy(s).wait_send()


def shards(l_blocks, s_blocks, l_index, s_cols, c_index):
    row_count = lax.axis_size("rows")
    own, kept = l_blocks.shape[0], c_index.shape[1]
    vmem, hbm = pl.BlockSpec(memory_space=pltpu.VMEM), pl.BlockSpec(memory_space=pl.ANY)
    return pl.pallas_call(
        functools.partial(kernel, row_count),
        out_shape=pltpu.VMEM((own, B, kept * B), jnp.bfloat16),
        in_specs=[hbm, hbm, vmem, vmem, vmem],
        out_specs=vmem,
        scratch_shapes=[
            pltpu.VMEM(s_blocks.shape, jnp.bfloat16),
            pltpu.VMEM(l_blocks.shape, jnp.bfloat16),
            pltpu.VMEM((CHUNKS, PARTS, TILES, B, 128), jnp.bfloat16),
            pltpu.VMEM((ZERO_S + 1, B, 128), jnp.bfloat16),
            pltpu.VMEM((4, 8 * B, 4 * B), jnp.bfloat16),
            pltpu.VMEM((ZERO_L + 1, B, 128), jnp.bfloat16),
            pltpu.VMEM((VIEW, own * B, 8 * B), jnp.bfloat16),
            pltpu.VMEM((2 * QUADS + 1, own * B, 128), jnp.float32),
            pltpu.VMEM((C_ROW + 8, 256), jnp.int32),
            pltpu.SMEM((C_ROW + 8, 256), jnp.int32),
            pltpu.SemaphoreType.DMA((20,)),
            pltpu.SemaphoreType.DMA((20,)),
            pltpu.SemaphoreType.DMA((3,)),
        ],
        compiler_params=pltpu.CompilerParams(
            collective_id=0, has_side_effects=True, vmem_limit_bytes=56 * 1024 * 1024
        ),
        cost_estimate=pl.CostEstimate(flops=4_700_000_000, bytes_accessed=5_000_000, transcendentals=0),
    )(s_blocks, l_blocks, l_index, s_cols.T, c_index)


def solution(mesh):
    return jax.shard_map(
        shards,
        mesh=mesh,
        in_specs=(
            P(("rows", "cols"), None, None),
            P("rows", None, "cols"),
            P(("rows", "cols"), None),
            P(),
            P(("rows", "cols"), None),
        ),
        out_specs=P(("rows", "cols"), None, None),
        check_vma=False,
    )
```

```python
import functools

import jax
import jax.numpy as jnp
from jax import lax
from jax.experimental import pallas as pl
from jax.experimental.pallas import tpu as pltpu
from jax.sharding import PartitionSpec as P

MESH = pl.DeviceIdType.MESH
B = 64
PARTS = 4
KSP = 5
SPAN = 8
TILES = 20
CHUNKS = 6
QUADS = 16
VIEW = 5
ZERO_S = 80
ZERO_L = 30
L_ROW, C_ROW = 32, 40
X0, A0, C0, E0, D0, F0, G0 = 0, 4, 8, 10, 12, 16, 18
LATE = 20
PIECE = TILES // 2


def place(row_count):
    r = lax.axis_index("rows")
    c = lax.axis_index("cols")
    x = c // 2
    outer = jnp.where(x == 0, (c == 0) & (r > 0), (c == 3) & (r < row_count - 1))
    skip = jnp.where(x == 0, jnp.where(outer, 0, 1), jnp.where(outer, 1, 0))
    first_quad = 8 * r - 4 * (1 - x) + 2 * skip
    return r, c, x, outer, skip, first_quad


def swap(v):
    return jnp.concatenate([v[:, B:], v[:, :B]], axis=1)


def kernel(
    row_count, s_hbm, l_hbm, li_hbm, sc_hbm, ci_hbm, out_ref,
    s_ref, l_ref, li_ref, sc_ref, ci_ref, near, table, dense_s, l_table, dense_l, total, codes, spots,
    send_sem, recv_sem, in_sem,
):
    r, c, x, outer, skip, first_quad = place(row_count)
    k = c % 2
    up, down = r < row_count - 1, r > 0
    has_next = jnp.where(x == 0, up, down)
    has_prev = jnp.where(x == 0, down, up)
    next_row = jnp.where(x == 0, r + 1, r - 1)
    core = (r, 2 * x + 1 - k)
    across = (r, 2 * (1 - x) + k)
    ahead = (next_row, c)
    mine, theirs = c, 2 * (1 - x) + k
    quad_count = 8 * row_count
    base_quad = jnp.clip(first_quad - 3, 0, quad_count - QUADS)

    barrier = pltpu.get_barrier_semaphore()
    pl.semaphore_signal(barrier, inc=1, device_id=core, device_id_type=MESH)
    pl.semaphore_signal(barrier, inc=1, device_id=across, device_id_type=MESH)

    @pl.when(up)
    def _():
        pl.semaphore_signal(barrier, inc=1, device_id=(r + 1, c), device_id_type=MESH)

    @pl.when(down)
    def _():
        pl.semaphore_signal(barrier, inc=1, device_id=(r - 1, c), device_id_type=MESH)

    def s_in(step):
        rows = pl.ds(8 * jnp.where(x == 0, step, 3 - step), 8)
        return pltpu.make_async_copy(s_hbm.at[rows], s_ref.at[rows], in_sem.at[step])

    for step in (0, 3, 1, 2):
        s_in(step).start()
    small_in = [
        pltpu.make_async_copy(source, target, in_sem.at[4 + n])
        for n, (source, target) in enumerate(((sc_hbm, sc_ref), (li_hbm, li_ref), (ci_hbm, ci_ref), (l_hbm, l_ref)))
    ]
    l_in = small_in.pop()
    for operand in small_in:
        operand.start()
    l_in.start()

    low = lax.broadcasted_iota(jnp.int32, (B, 128), 1) < B
    low16 = lax.broadcasted_iota(jnp.int16, (B, 128), 1) < B

    def flip(t):
        return jnp.where(x == 1, t, 5 - t)

    def copy(src_chunk, dst_chunk, part, index, device, piece=None):
        tiles = slice(None) if piece is None else pl.ds(piece * PIECE, PIECE)
        index = index if not piece else LATE + (index - X0) // 4
        return pltpu.make_async_remote_copy(
            src_ref=near.at[src_chunk, part, tiles],
            dst_ref=near.at[dst_chunk, part, tiles],
            send_sem=send_sem.at[index],
            recv_sem=recv_sem.at[index],
            device_id=device,
            device_id_type=MESH,
        )

    def x_copy(s, piece=None):
        source, target = jnp.where(x == 0, s + 2, 3 - s), jnp.where(x == 0, s, 5 - s)
        return copy(source, target, mine, X0 + s, across, piece)

    def a_copy(s):
        return copy(flip(s), flip(s), mine, A0 + s, core)

    def c_copy(s):
        return copy(flip(s), flip(4 + s), mine, C0 + s, ahead)

    def e_copy(s, piece=None):
        return copy(flip(s), flip(4 + s), theirs, E0 + s, ahead, piece)

    def d_copy(s, piece=None):
        return copy(flip(s), flip(s), theirs, D0 + s, core, piece)

    def f_copy(s):
        return copy(flip(4 + s), flip(4 + s), mine, F0 + s, core)

    def g_copy(s, piece=None):
        return copy(flip(4 + s), flip(4 + s), theirs, G0 + s, core, piece)

    def pieces(s, last):
        return (0, 1) if s == last else (None,)

    for step in (0, 3, 1, 2):
        group_chunk = jnp.where(x == 0, step, 3 - step)
        chunk = group_chunk + 2 * (1 - x)
        s_in(step).wait()

        @pl.loop(0, 4)
        def _(pair):
            at = pair * 5
            source = 8 * group_chunk + 2 * pair
            for odd in range(2):
                for t in range(2):
                    near[chunk, mine, at + 2 * odd + t] = s_ref[source + odd, :, t * 128 : t * 128 + 128]
            near[chunk, mine, at + 4] = jnp.concatenate(
                [s_ref[source, :, 256:320], s_ref[source + 1, :, 256:320]], axis=1
            )

        if step == 0:
            pl.semaphore_wait(barrier, 2 + up.astype(jnp.int32) + down.astype(jnp.int32))
        if step < 2:
            x_copy(step).start()
        else:

            @pl.when(has_next)
            def _():
                c_copy(3 - step).start()

        a_copy(3 - step).start()

    for operand in small_in:
        operand.wait()
    base_row = 128 * jnp.clip(4 * first_quad // 128, 0, 4 * quad_count // 128 - 2)
    cols = sc_ref[:, pl.ds(pl.multiple_of(base_row, 128), 256)]
    want_at = lax.broadcasted_iota(jnp.int32, (4 * SPAN, 256), 0)
    row = lax.broadcasted_iota(jnp.int32, (4 * SPAN, 256), 1)
    odd, side = row % 2, want_at % 2
    want = 4 * jnp.clip(2 * ((base_row + row) // 8) - 3, 0, quad_count - SPAN) + want_at
    first_tile = ((row // 2) % 4) * 5
    code = jnp.full((4 * SPAN, 256), ZERO_S, jnp.int32)
    for within in range(KSP):
        if within < 4:
            tile = first_tile + 2 * odd + within // 2 + jnp.where(side != within % 2, 40, 0)
        else:
            tile = first_tile + 4 + jnp.where(side != odd, 40, 0)
        for part in range(PARTS):
            slot = part * KSP + within
            code = jnp.where(cols[slot : slot + 1, :] == want, tile + (part % 2) * TILES, code)
    codes[0 : 4 * SPAN, :] = code
    lane = lax.broadcasted_iota(jnp.int32, (8, 256), 1)
    side = lane % 2
    want = jnp.where(lane < 8 * VIEW, 4 * first_quad + lane, -1)
    code = jnp.full((8, 256), ZERO_L, jnp.int32)
    for slot in range(30):
        tile = slot // 2 + jnp.where(side != slot % 2, 15, 0)
        code = jnp.where(li_ref[:, slot : slot + 1] == want, tile, code)
    codes[L_ROW : L_ROW + 8, :] = code
    codes[C_ROW : C_ROW + 8, :] = jnp.zeros((8, 256), jnp.int32)
    spot = ci_ref[...] - 4 * base_quad
    codes[C_ROW : C_ROW + 8, 0 : spot.shape[1]] = jnp.where((spot >= 0) & (spot < 4 * QUADS), spot, 4 * QUADS)
    down_copy = pltpu.make_async_copy(codes, spots, in_sem.at[8])
    down_copy.start()

    @pl.loop(0, 2 * QUADS + 1)
    def _(q):
        total[q] = jnp.zeros(total.shape[1:], jnp.float32)

    table[ZERO_S] = jnp.zeros((B, 128), jnp.bfloat16)
    l_table[ZERO_L] = jnp.zeros((B, 128), jnp.bfloat16)
    down_copy.wait()
    l_in.wait()

    @pl.loop(0, 8)
    def _(i):
        for t in range(15):
            v = l_ref[i, :, t * 128 : t * 128 + 128]
            l_table[t] = v
            l_table[15 + t] = swap(v)
        rows = pl.ds(pl.multiple_of(i * B, B), B)
        for g in range(VIEW):
            for at in range(4):
                spot = 8 * g + 2 * at
                dense_l[g, rows, at * 128 : at * 128 + 128] = jnp.where(
                    low16, l_table[spots[L_ROW + i, spot]], l_table[spots[L_ROW + i, spot + 1]]
                )

    def multiply(chunk, half, piece=None):
        view = chunk - skip
        tiles = range(TILES) if piece is None else range(piece * PIECE, piece * PIECE + PIECE)
        near_rows = range(8) if piece is None else range(4 * piece, 4 * piece + 4)
        depth = slice(near_rows[0] * B, near_rows[-1] * B + B)

        @pl.loop(0, 2)
        def _(p):
            for t in tiles:
                v = near[chunk, 2 * half + p, t]
                table[p * TILES + t] = v
                table[40 + p * TILES + t] = swap(v)

        start = jnp.clip(first_quad + 2 * view - 3, 0, quad_count - SPAN) - base_quad
        first = 4 * first_quad - base_row + view * 8

        for n in range(4):
            for row in near_rows:
                for w in range(2):
                    spot = 8 * n + 4 * w + 2 * half
                    dense_s[n, row * B : row * B + B, w * 128 : w * 128 + 128] = jnp.where(
                        low16, table[spots[spot, first + row]], table[spots[spot + 1, first + row]]
                    )
            part = jnp.dot(dense_l[view, :, depth], dense_s[n, depth, :], preferred_element_type=jnp.float32)
            at = 2 * (start + 2 * n) + half
            total[at] += part[:, :128]
            total[at + 2] += part[:, 128:]

    events = ("A0", "A1", "X0", "C0", "A2", "X1", "C1", "A3", "E0", "X2")

    def when_prev(action):
        pl.when(has_prev)(action)

    def used(order):
        return jnp.where(outer, order != 0, order != 5) & (has_prev | (order < 4))

    def arrive_x(s):
        x_copy(s).wait_recv()
        if s < 2:
            for piece in pieces(s, 1):
                pl.when(has_next)(lambda: e_copy(s, piece).start())
                x_copy(s + 2, piece).start()
        d_copy(s).start()

    def arrive_c(s):
        c_copy(s).wait_recv()
        f_copy(s).start()

    def arrive_e(s, piece=None):
        e_copy(s, piece).wait_recv()
        g_copy(s, piece).start()

    def before(kind, s):
        if kind == "A":
            a_copy(s).wait_recv()
        elif kind == "X":
            if s < 2:
                arrive_x(s)
                when_prev(lambda: arrive_c(s))
            d_copy(s).wait_recv()
        elif kind == "C":
            when_prev(lambda: f_copy(s).wait_recv())
        else:
            when_prev(lambda: arrive_e(s))
            arrive_x(2)
            when_prev(lambda: g_copy(s).wait_recv())

    @pl.loop(0, len(events))
    def _(e):
        order, own_half = e * 0, e * 0
        for index, (kind, s) in enumerate(events):
            order = jnp.where(e == index, int(s) if kind in "AX" else 4 + int(s), order)
            own_half = jnp.where(e == index, 1 if kind in "AC" else 0, own_half)
            pl.when(e == index)(functools.partial(before, kind, int(s)))

        @pl.when(used(order))
        def _():
            multiply(flip(order), jnp.where(own_half == 1, x, 1 - x))

    for piece in range(2):
        x_copy(3, piece).wait_recv()
        d_copy(3, piece).start()
        when_prev(lambda: arrive_e(1, piece))

        @pl.loop(0, 2)
        def _(e):
            pl.when(e == 0)(lambda: d_copy(3, piece).wait_recv())
            pl.when((e == 1) & has_prev)(lambda: g_copy(1, piece).wait_recv())
            order = 3 + 2 * e

            @pl.when(used(order))
            def _():
                multiply(flip(order), 1 - x, piece)

    @pl.loop(0, 8)
    def _(i):
        rows = pl.ds(pl.multiple_of(i * B, B), B)
        for m in range(12):
            left, right = spots[C_ROW + i, 2 * m], spots[C_ROW + i, 2 * m + 1]
            a, b = total[left // 2, rows, :], total[right // 2, rows, :]
            straight = jnp.where(low, a, b)
            crossed = pltpu.roll(jnp.where(low, b, a), B, 1)
            keep = jnp.where(low, 1 - left % 2, right % 2) == 1
            out_ref[i, :, m * 128 : m * 128 + 128] = jnp.where(keep, straight, crossed).astype(jnp.bfloat16)

    for s in range(4):
        a_copy(s).wait_send()
        for piece in pieces(s, 3):
            x_copy(s, piece).wait_send()
            d_copy(s, piece).wait_send()
    for s in range(2):

        @pl.when(has_next)
        def _():
            c_copy(s).wait_send()
            for piece in pieces(s, 1):
                e_copy(s, piece).wait_send()

        @pl.when(has_prev)
        def _():
            f_copy(s).wait_send()
            for piece in pieces(s, 1):
                g_copy(s, piece).wait_send()


def shards(l_blocks, s_blocks, l_index, s_cols, c_index):
    row_count = lax.axis_size("rows")
    own, kept = l_blocks.shape[0], c_index.shape[1]
    vmem, hbm = pl.BlockSpec(memory_space=pltpu.VMEM), pl.BlockSpec(memory_space=pl.ANY)
    return pl.pallas_call(
        functools.partial(kernel, row_count),
        out_shape=pltpu.VMEM((own, B, kept * B), jnp.bfloat16),
        in_specs=[hbm] * 5,
        out_specs=vmem,
        scratch_shapes=[
            pltpu.VMEM(s_blocks.shape, jnp.bfloat16),
            pltpu.VMEM(l_blocks.shape, jnp.bfloat16),
            pltpu.VMEM(l_index.shape, jnp.int32),
            pltpu.VMEM(s_cols.shape[::-1], jnp.int32),
            pltpu.VMEM(c_index.shape, jnp.int32),
            pltpu.VMEM((CHUNKS, PARTS, TILES, B, 128), jnp.bfloat16),
            pltpu.VMEM((ZERO_S + 1, B, 128), jnp.bfloat16),
            pltpu.VMEM((4, 8 * B, 4 * B), jnp.bfloat16),
            pltpu.VMEM((ZERO_L + 1, B, 128), jnp.bfloat16),
            pltpu.VMEM((VIEW, own * B, 8 * B), jnp.bfloat16),
            pltpu.VMEM((2 * QUADS + 1, own * B, 128), jnp.float32),
            pltpu.VMEM((C_ROW + 8, 256), jnp.int32),
            pltpu.SMEM((C_ROW + 8, 256), jnp.int32),
            pltpu.SemaphoreType.DMA((LATE + 5,)),
            pltpu.SemaphoreType.DMA((LATE + 5,)),
            pltpu.SemaphoreType.DMA((9,)),
        ],
        compiler_params=pltpu.CompilerParams(
            collective_id=0, has_side_effects=True, vmem_limit_bytes=56 * 1024 * 1024
        ),
        cost_estimate=pl.CostEstimate(flops=4_700_000_000, bytes_accessed=5_000_000, transcendentals=0),
    )(s_blocks, l_blocks, l_index, s_cols.T, c_index)


def solution(mesh):
    return jax.shard_map(
        shards,
        mesh=mesh,
        in_specs=(
            P(("rows", "cols"), None, None),
            P("rows", None, "cols"),
            P(("rows", "cols"), None),
            P(),
            P(("rows", "cols"), None),
        ),
        out_specs=P(("rows", "cols"), None, None),
        check_vma=False,
    )
```

```python
import functools

import jax
import jax.numpy as jnp
from jax import lax
from jax.experimental import pallas as pl
from jax.experimental.pallas import tpu as pltpu
from jax.sharding import PartitionSpec as P

MESH = pl.DeviceIdType.MESH
B = 64
PARTS = 4
KSP = 5
SPAN = 8
TILES = 20
CHUNKS = 6
QUADS = 16
VIEW = 5
ZERO_S = 80
ZERO_L = 30
L_ROW, C_ROW = 32, 40
X0, A0, C0, E0, D0, F0, G0 = 0, 4, 8, 10, 12, 16, 18
LATE = 20
PIECE = TILES // 2


def place(row_count):
    r = lax.axis_index("rows")
    c = lax.axis_index("cols")
    x = c // 2
    outer = jnp.where(x == 0, (c == 0) & (r > 0), (c == 3) & (r < row_count - 1))
    skip = jnp.where(x == 0, jnp.where(outer, 0, 1), jnp.where(outer, 1, 0))
    first_quad = 8 * r - 4 * (1 - x) + 2 * skip
    return r, c, x, outer, skip, first_quad


def swap(v):
    return jnp.concatenate([v[:, B:], v[:, :B]], axis=1)


def kernel(
    row_count, s_hbm, l_hbm, li_hbm, sc_hbm, ci_hbm, out_ref,
    s_ref, l_ref, li_ref, sc_ref, ci_ref, near, table, dense_s, l_table, dense_l, total, codes, spots,
    send_sem, recv_sem, in_sem,
):
    r, c, x, outer, skip, first_quad = place(row_count)
    k = c % 2
    up, down = r < row_count - 1, r > 0
    has_next = jnp.where(x == 0, up, down)
    has_prev = jnp.where(x == 0, down, up)
    next_row = jnp.where(x == 0, r + 1, r - 1)
    core = (r, 2 * x + 1 - k)
    across = (r, 2 * (1 - x) + k)
    ahead = (next_row, c)
    mine, theirs = c, 2 * (1 - x) + k
    quad_count = 8 * row_count
    base_quad = jnp.clip(first_quad - 3, 0, quad_count - QUADS)

    barrier = pltpu.get_barrier_semaphore()
    pl.semaphore_signal(barrier, inc=1, device_id=core, device_id_type=MESH)
    pl.semaphore_signal(barrier, inc=1, device_id=across, device_id_type=MESH)

    @pl.when(up)
    def _():
        pl.semaphore_signal(barrier, inc=1, device_id=(r + 1, c), device_id_type=MESH)

    @pl.when(down)
    def _():
        pl.semaphore_signal(barrier, inc=1, device_id=(r - 1, c), device_id_type=MESH)

    def s_in(step):
        rows = pl.ds(8 * jnp.where(x == 0, step, 3 - step), 8)
        return pltpu.make_async_copy(s_hbm.at[rows], s_ref.at[rows], in_sem.at[step])

    for step in (0, 3, 1, 2):
        s_in(step).start()
    small_in = [
        pltpu.make_async_copy(source, target, in_sem.at[4 + n])
        for n, (source, target) in enumerate(((sc_hbm, sc_ref), (li_hbm, li_ref), (ci_hbm, ci_ref), (l_hbm, l_ref)))
    ]
    l_in = small_in.pop()
    for operand in small_in:
        operand.start()
    l_in.start()

    low = lax.broadcasted_iota(jnp.int32, (B, 128), 1) < B
    low16 = lax.broadcasted_iota(jnp.int16, (B, 128), 1) < B

    def flip(t):
        return jnp.where(x == 1, t, 5 - t)

    def copy(src_chunk, dst_chunk, part, index, device, piece=None, trim=False, near_quad=1 - x):
        if piece is None:
            tiles = pl.ds(2 * (1 - x), TILES - 2) if trim else slice(None)
        elif piece == 0:
            tiles = pl.ds(PIECE * near_quad, PIECE)
        else:
            tiles = pl.ds(2 + 8 * x, PIECE - 2) if trim else pl.ds(PIECE * (1 - near_quad), PIECE)
        index = index if not piece else LATE + (index - X0) // 4
        return pltpu.make_async_remote_copy(
            src_ref=near.at[src_chunk, part, tiles],
            dst_ref=near.at[dst_chunk, part, tiles],
            send_sem=send_sem.at[index],
            recv_sem=recv_sem.at[index],
            device_id=device,
            device_id_type=MESH,
        )

    def x_copy(s, piece=None):
        source, target = jnp.where(x == 0, s + 2, 3 - s), jnp.where(x == 0, s, 5 - s)
        return copy(source, target, mine, X0 + s, across, piece, near_quad=x)

    def a_copy(s):
        return copy(flip(s), flip(s), mine, A0 + s, core)

    def c_copy(s):
        return copy(flip(s), flip(4 + s), mine, C0 + s, ahead, trim=s == 1)

    def e_copy(s, piece=None):
        return copy(flip(s), flip(4 + s), theirs, E0 + s, ahead, piece, trim=s == 1)

    def d_copy(s, piece=None):
        return copy(flip(s), flip(s), theirs, D0 + s, core, piece)

    def f_copy(s):
        return copy(flip(4 + s), flip(4 + s), mine, F0 + s, core, trim=s == 1)

    def g_copy(s, piece=None):
        return copy(flip(4 + s), flip(4 + s), theirs, G0 + s, core, piece, trim=s == 1)

    def pieces(s, last):
        return (0, 1) if s == last else (None,)

    for step in (0, 3, 1, 2):
        group_chunk = jnp.where(x == 0, step, 3 - step)
        chunk = group_chunk + 2 * (1 - x)
        s_in(step).wait()

        @pl.loop(0, 4)
        def _(pair):
            at = pair * 5
            source = 8 * group_chunk + 2 * pair
            for odd in range(2):
                for t in range(2):
                    near[chunk, mine, at + 3 * odd + t] = s_ref[source + odd, :, t * 128 : t * 128 + 128]
            near[chunk, mine, at + 2] = jnp.concatenate(
                [s_ref[source, :, 256:320], s_ref[source + 1, :, 256:320]], axis=1
            )

        if step == 0:
            pl.semaphore_wait(barrier, 2 + up.astype(jnp.int32) + down.astype(jnp.int32))
        if step < 2:
            x_copy(step).start()
        else:

            @pl.when(has_next)
            def _():
                c_copy(3 - step).start()

        a_copy(3 - step).start()

    for operand in small_in:
        operand.wait()
    base_row = 128 * jnp.clip(4 * first_quad // 128, 0, 4 * quad_count // 128 - 2)
    cols = sc_ref[:, pl.ds(pl.multiple_of(base_row, 128), 256)]
    want_at = lax.broadcasted_iota(jnp.int32, (4 * SPAN, 256), 0)
    row = lax.broadcasted_iota(jnp.int32, (4 * SPAN, 256), 1)
    odd, side = row % 2, want_at % 2
    want = 4 * jnp.clip(2 * ((base_row + row) // 8) - 3, 0, quad_count - SPAN) + want_at
    want = jnp.where(base_row + row == 32 * r + jnp.where(x == 0, -16, 47), -1, want)
    first_tile = ((row // 2) % 4) * 5
    code = jnp.full((4 * SPAN, 256), ZERO_S, jnp.int32)
    for within in range(KSP):
        if within < 4:
            tile = first_tile + 3 * odd + within // 2 + jnp.where(side != within % 2, 40, 0)
        else:
            tile = first_tile + 2 + jnp.where(side != odd, 40, 0)
        for part in range(PARTS):
            slot = part * KSP + within
            code = jnp.where(cols[slot : slot + 1, :] == want, tile + (part % 2) * TILES, code)
    codes[0 : 4 * SPAN, :] = code
    lane = lax.broadcasted_iota(jnp.int32, (8, 256), 1)
    side = lane % 2
    want = jnp.where(lane < 8 * VIEW, 4 * first_quad + lane, -1)
    code = jnp.full((8, 256), ZERO_L, jnp.int32)
    for slot in range(30):
        tile = slot // 2 + jnp.where(side != slot % 2, 15, 0)
        code = jnp.where(li_ref[:, slot : slot + 1] == want, tile, code)
    codes[L_ROW : L_ROW + 8, :] = code
    codes[C_ROW : C_ROW + 8, :] = jnp.zeros((8, 256), jnp.int32)
    spot = ci_ref[...] - 4 * base_quad
    codes[C_ROW : C_ROW + 8, 0 : spot.shape[1]] = jnp.where((spot >= 0) & (spot < 4 * QUADS), spot, 4 * QUADS)
    down_copy = pltpu.make_async_copy(codes, spots, in_sem.at[8])
    down_copy.start()

    @pl.loop(0, 2 * QUADS + 1)
    def _(q):
        total[q] = jnp.zeros(total.shape[1:], jnp.float32)

    table[ZERO_S] = jnp.zeros((B, 128), jnp.bfloat16)
    l_table[ZERO_L] = jnp.zeros((B, 128), jnp.bfloat16)
    down_copy.wait()
    l_in.wait()

    @pl.loop(0, 8)
    def _(i):
        for t in range(15):
            v = l_ref[i, :, t * 128 : t * 128 + 128]
            l_table[t] = v
            l_table[15 + t] = swap(v)
        rows = pl.ds(pl.multiple_of(i * B, B), B)
        for g in range(VIEW):
            for at in range(4):
                spot = 8 * g + 2 * at
                dense_l[g, rows, at * 128 : at * 128 + 128] = jnp.where(
                    low16, l_table[spots[L_ROW + i, spot]], l_table[spots[L_ROW + i, spot + 1]]
                )

    def multiply(chunk, half, quad=None):
        view = chunk - skip
        if quad is None:
            near_rows, tile_count, tile_first = 8, TILES, 0
            left = dense_l.at[view]
        else:
            near_rows, tile_count, tile_first = 4, PIECE, PIECE * quad
            left = dense_l.at[view, :, pl.ds(pl.multiple_of(4 * B * quad, 4 * B), 4 * B)]
        depth = slice(0, near_rows * B)

        @pl.loop(0, 2)
        def _(p):
            for t in range(tile_count):
                at = tile_first + t
                v = near[chunk, 2 * half + p, at]
                table[p * TILES + at] = v
                table[40 + p * TILES + at] = swap(v)

        start = jnp.clip(first_quad + 2 * view - 3, 0, quad_count - SPAN) - base_quad
        first = 4 * first_quad - base_row + view * 8 + (0 if quad is None else 4 * quad)

        for n in range(4):
            for row in range(near_rows):
                for w in range(2):
                    spot = 8 * n + 4 * w + 2 * half
                    dense_s[n, row * B : row * B + B, w * 128 : w * 128 + 128] = jnp.where(
                        low16, table[spots[spot, first + row]], table[spots[spot + 1, first + row]]
                    )
            part = jnp.dot(left[...], dense_s[n, depth, :], preferred_element_type=jnp.float32)
            at = 2 * (start + 2 * n) + half
            total[at] += part[:, :128]
            total[at + 2] += part[:, 128:]

    events = ("A0", "A1", "X0", "C0", "A2", "X1", "C1", "A3", "E0", "X2")

    def when_prev(action):
        pl.when(has_prev)(action)

    def used(order):
        return jnp.where(outer, order != 0, order != 5) & (has_prev | (order < 4))

    def arrive_x(s):
        x_copy(s).wait_recv()
        if s < 2:
            for piece in pieces(s, 1):
                pl.when(has_next)(lambda: e_copy(s, piece).start())
                x_copy(s + 2, piece).start()
        d_copy(s).start()

    def arrive_c(s):
        c_copy(s).wait_recv()
        f_copy(s).start()

    def arrive_e(s, piece=None):
        e_copy(s, piece).wait_recv()
        g_copy(s, piece).start()

    def before(kind, s):
        if kind == "A":
            a_copy(s).wait_recv()
        elif kind == "X":
            if s < 2:
                arrive_x(s)
                when_prev(lambda: arrive_c(s))
            d_copy(s).wait_recv()
        elif kind == "C":
            when_prev(lambda: f_copy(s).wait_recv())
        else:
            when_prev(lambda: arrive_e(s))
            arrive_x(2)
            when_prev(lambda: g_copy(s).wait_recv())

    @pl.loop(0, len(events))
    def _(e):
        order, own_half = e * 0, e * 0
        for index, (kind, s) in enumerate(events):
            order = jnp.where(e == index, int(s) if kind in "AX" else 4 + int(s), order)
            own_half = jnp.where(e == index, 1 if kind in "AC" else 0, own_half)
            pl.when(e == index)(functools.partial(before, kind, int(s)))

        @pl.when(used(order))
        def _():
            multiply(flip(order), jnp.where(own_half == 1, x, 1 - x))

    def pick(half):
        @pl.loop(0, 8)
        def _(i):
            rows = pl.ds(pl.multiple_of(i * B, B), B)
            for m in range(6):
                slot = 12 * half + 2 * m
                left, right = spots[C_ROW + i, slot], spots[C_ROW + i, slot + 1]
                a, b = total[left // 2, rows, :], total[right // 2, rows, :]
                straight = jnp.where(low, a, b)
                crossed = pltpu.roll(jnp.where(low, b, a), B, 1)
                keep = jnp.where(low, 1 - left % 2, right % 2) == 1
                at = pl.ds(pl.multiple_of(slot * B, 2 * B), 2 * B)
                out_ref[i, :, at] = jnp.where(keep, straight, crossed).astype(jnp.bfloat16)

    pick(x)

    for piece in range(2):
        x_copy(3, piece).wait_recv()
        d_copy(3, piece).start()
        when_prev(lambda: arrive_e(1, piece))

        @pl.loop(0, 2)
        def _(e):
            pl.when(e == 0)(lambda: d_copy(3, piece).wait_recv())
            pl.when((e == 1) & has_prev)(lambda: g_copy(1, piece).wait_recv())
            order = 3 + 2 * e

            @pl.when(used(order))
            def _():
                multiply(flip(order), 1 - x, 1 - x if piece == 0 else x)

    pick(1 - x)

    for s in range(4):
        a_copy(s).wait_send()
        for piece in pieces(s, 3):
            x_copy(s, piece).wait_send()
            d_copy(s, piece).wait_send()
    for s in range(2):

        @pl.when(has_next)
        def _():
            c_copy(s).wait_send()
            for piece in pieces(s, 1):
                e_copy(s, piece).wait_send()

        @pl.when(has_prev)
        def _():
            f_copy(s).wait_send()
            for piece in pieces(s, 1):
                g_copy(s, piece).wait_send()


def shards(l_blocks, s_blocks, l_index, s_cols, c_index):
    row_count = lax.axis_size("rows")
    own, kept = l_blocks.shape[0], c_index.shape[1]
    vmem, hbm = pl.BlockSpec(memory_space=pltpu.VMEM), pl.BlockSpec(memory_space=pl.ANY)
    return pl.pallas_call(
        functools.partial(kernel, row_count),
        out_shape=pltpu.VMEM((own, B, kept * B), jnp.bfloat16),
        in_specs=[hbm] * 5,
        out_specs=vmem,
        scratch_shapes=[
            pltpu.VMEM(s_blocks.shape, jnp.bfloat16),
            pltpu.VMEM(l_blocks.shape, jnp.bfloat16),
            pltpu.VMEM(l_index.shape, jnp.int32),
            pltpu.VMEM(s_cols.shape[::-1], jnp.int32),
            pltpu.VMEM(c_index.shape, jnp.int32),
            pltpu.VMEM((CHUNKS, PARTS, TILES, B, 128), jnp.bfloat16),
            pltpu.VMEM((ZERO_S + 1, B, 128), jnp.bfloat16),
            pltpu.VMEM((4, 8 * B, 4 * B), jnp.bfloat16),
            pltpu.VMEM((ZERO_L + 1, B, 128), jnp.bfloat16),
            pltpu.VMEM((VIEW, own * B, 8 * B), jnp.bfloat16),
            pltpu.VMEM((2 * QUADS + 1, own * B, 128), jnp.float32),
            pltpu.VMEM((C_ROW + 8, 256), jnp.int32),
            pltpu.SMEM((C_ROW + 8, 256), jnp.int32),
            pltpu.SemaphoreType.DMA((LATE + 5,)),
            pltpu.SemaphoreType.DMA((LATE + 5,)),
            pltpu.SemaphoreType.DMA((9,)),
        ],
        compiler_params=pltpu.CompilerParams(
            collective_id=0, has_side_effects=True, vmem_limit_bytes=56 * 1024 * 1024
        ),
        cost_estimate=pl.CostEstimate(flops=4_700_000_000, bytes_accessed=5_000_000, transcendentals=0),
    )(s_blocks, l_blocks, l_index, s_cols.T, c_index)


def solution(mesh):
    return jax.shard_map(
        shards,
        mesh=mesh,
        in_specs=(
            P(("rows", "cols"), None, None),
            P("rows", None, "cols"),
            P(("rows", "cols"), None),
            P(),
            P(("rows", "cols"), None),
        ),
        out_specs=P(("rows", "cols"), None, None),
        check_vma=False,
    )
```

```python
import functools

import jax
import jax.numpy as jnp
from jax import lax
from jax.experimental import pallas as pl
from jax.experimental.pallas import tpu as pltpu
from jax.sharding import PartitionSpec as P

MESH = pl.DeviceIdType.MESH
B = 64
PARTS = 4
KSP = 5
SPAN = 8
TILES = 20
CHUNKS = 6
QUADS = 16
VIEW = 5
ZERO_S = 80
ZERO_L = 30
L_ROW, C_ROW = 32, 40
X0, A0, C0, E0, D0, F0, G0 = 0, 4, 8, 10, 12, 16, 18
LATE = 20
PIECE = TILES // 2


def place(row_count):
    r = lax.axis_index("rows")
    c = lax.axis_index("cols")
    x = c // 2
    outer = jnp.where(x == 0, (c == 0) & (r > 0), (c == 3) & (r < row_count - 1))
    skip = jnp.where(x == 0, jnp.where(outer, 0, 1), jnp.where(outer, 1, 0))
    first_quad = 8 * r - 4 * (1 - x) + 2 * skip
    return r, c, x, outer, skip, first_quad


def swap(v):
    return jnp.concatenate([v[:, B:], v[:, :B]], axis=1)


def kernel(
    row_count, s_hbm, l_hbm, li_hbm, sc_hbm, ci_hbm, out_ref,
    s_ref, l_ref, li_ref, sc_ref, ci_ref, near, table, dense_s, l_table, dense_l, total, codes, spots,
    send_sem, recv_sem, in_sem,
):
    r, c, x, outer, skip, first_quad = place(row_count)
    k = c % 2
    up, down = r < row_count - 1, r > 0
    has_next = jnp.where(x == 0, up, down)
    has_prev = jnp.where(x == 0, down, up)
    next_row = jnp.where(x == 0, r + 1, r - 1)
    core = (r, 2 * x + 1 - k)
    across = (r, 2 * (1 - x) + k)
    ahead = (next_row, c)
    ahead_outer = (next_row, 3 * x)
    outer_core = k == x
    mine, theirs = c, 2 * (1 - x) + k
    quad_count = 8 * row_count
    base_quad = jnp.clip(first_quad - 3, 0, quad_count - QUADS)

    barrier = pltpu.get_barrier_semaphore()
    pl.semaphore_signal(barrier, inc=1, device_id=core, device_id_type=MESH)
    pl.semaphore_signal(barrier, inc=1, device_id=across, device_id_type=MESH)

    @pl.when(up)
    def _():
        pl.semaphore_signal(barrier, inc=1, device_id=(r + 1, c), device_id_type=MESH)
        pl.semaphore_signal(barrier, inc=1, device_id=(r + 1, 2 * x + 1 - k), device_id_type=MESH)

    @pl.when(down)
    def _():
        pl.semaphore_signal(barrier, inc=1, device_id=(r - 1, c), device_id_type=MESH)
        pl.semaphore_signal(barrier, inc=1, device_id=(r - 1, 2 * x + 1 - k), device_id_type=MESH)

    def s_in(step):
        rows = pl.ds(8 * jnp.where(x == 0, step, 3 - step), 8)
        return pltpu.make_async_copy(s_hbm.at[rows], s_ref.at[rows], in_sem.at[step])

    for step in (0, 3, 1, 2):
        s_in(step).start()
    small_in = [
        pltpu.make_async_copy(source, target, in_sem.at[4 + n])
        for n, (source, target) in enumerate(((sc_hbm, sc_ref), (li_hbm, li_ref), (ci_hbm, ci_ref), (l_hbm, l_ref)))
    ]
    l_in = small_in.pop()
    for operand in small_in:
        operand.start()
    l_in.start()

    low = lax.broadcasted_iota(jnp.int32, (B, 128), 1) < B
    low16 = lax.broadcasted_iota(jnp.int16, (B, 128), 1) < B

    def flip(t):
        return jnp.where(x == 1, t, 5 - t)

    def copy(src_chunk, dst_chunk, part, index, device, piece=None, trim=False, near_quad=1 - x):
        if piece is None:
            tiles = pl.ds(2 * (1 - x), TILES - 2) if trim else slice(None)
        elif piece == 0:
            tiles = pl.ds(PIECE * near_quad, PIECE)
        else:
            tiles = pl.ds(2 + 8 * x, PIECE - 2) if trim else pl.ds(PIECE * (1 - near_quad), PIECE)
        index = LATE + (index - X0) // 4 if piece else index
        return pltpu.make_async_remote_copy(
            src_ref=near.at[src_chunk, part, tiles],
            dst_ref=near.at[dst_chunk, part, tiles],
            send_sem=send_sem.at[index],
            recv_sem=recv_sem.at[index],
            device_id=device,
            device_id_type=MESH,
        )

    def x_copy(s, piece=None):
        source, target = jnp.where(x == 0, s + 2, 3 - s), jnp.where(x == 0, s, 5 - s)
        return copy(source, target, mine, X0 + s, across, piece, near_quad=x)

    def a_copy(s):
        return copy(flip(s), flip(s), mine, A0 + s, core)

    def c_copy(s):
        if s == 1:
            return copy(flip(1), flip(5), mine, jnp.where(outer_core, C0 + 1, F0 + 1), ahead_outer, trim=True)
        return copy(flip(s), flip(4 + s), mine, C0 + s, ahead)

    def e_copy(s, piece=None):
        if s == 1:
            index = jnp.where(outer_core, E0 + 1, G0 + 1)
            return copy(flip(1), flip(5), theirs, index, ahead_outer, piece, trim=True)
        return copy(flip(s), flip(4 + s), theirs, E0 + s, ahead)

    def d_copy(s, piece=None):
        return copy(flip(s), flip(s), theirs, D0 + s, core, piece)

    def f_copy(s):
        return copy(flip(4 + s), flip(4 + s), mine, F0 + s, core, trim=s == 1)

    def g_copy(s, piece=None):
        return copy(flip(4 + s), flip(4 + s), theirs, G0 + s, core, piece, trim=s == 1)

    def pieces(s, last):
        return (0, 1) if s == last else (None,)

    for step in (0, 3, 1, 2):
        group_chunk = jnp.where(x == 0, step, 3 - step)
        chunk = group_chunk + 2 * (1 - x)
        s_in(step).wait()

        @pl.loop(0, 4)
        def _(pair):
            at = pair * 5
            source = 8 * group_chunk + 2 * pair
            for odd in range(2):
                for t in range(2):
                    near[chunk, mine, at + 3 * odd + t] = s_ref[source + odd, :, t * 128 : t * 128 + 128]
            near[chunk, mine, at + 2] = jnp.concatenate(
                [s_ref[source, :, 256:320], s_ref[source + 1, :, 256:320]], axis=1
            )

        if step == 0:
            pl.semaphore_wait(barrier, 2 + 2 * up.astype(jnp.int32) + 2 * down.astype(jnp.int32))
        if step < 2:
            x_copy(step).start()
        else:

            @pl.when(has_next)
            def _():
                c_copy(3 - step).start()

        a_copy(3 - step).start()

    for operand in small_in:
        operand.wait()
    base_row = 128 * jnp.clip(4 * first_quad // 128, 0, 4 * quad_count // 128 - 2)
    cols = sc_ref[:, pl.ds(pl.multiple_of(base_row, 128), 256)]
    want_at = lax.broadcasted_iota(jnp.int32, (4 * SPAN, 256), 0)
    row = lax.broadcasted_iota(jnp.int32, (4 * SPAN, 256), 1)
    odd, side = row % 2, want_at % 2
    want = 4 * jnp.clip(2 * ((base_row + row) // 8) - 3, 0, quad_count - SPAN) + want_at
    want = jnp.where(base_row + row == 32 * r + jnp.where(x == 0, -16, 47), -1, want)
    first_tile = ((row // 2) % 4) * 5
    code = jnp.full((4 * SPAN, 256), ZERO_S, jnp.int32)
    for within in range(KSP):
        if within < 4:
            tile = first_tile + 3 * odd + within // 2 + jnp.where(side != within % 2, 40, 0)
        else:
            tile = first_tile + 2 + jnp.where(side != odd, 40, 0)
        for part in range(PARTS):
            slot = part * KSP + within
            code = jnp.where(cols[slot : slot + 1, :] == want, tile + (part % 2) * TILES, code)
    codes[0 : 4 * SPAN, :] = code
    lane = lax.broadcasted_iota(jnp.int32, (8, 256), 1)
    side = lane % 2
    want = jnp.where(lane < 8 * VIEW, 4 * first_quad + lane, -1)
    code = jnp.full((8, 256), ZERO_L, jnp.int32)
    for slot in range(30):
        tile = slot // 2 + jnp.where(side != slot % 2, 15, 0)
        code = jnp.where(li_ref[:, slot : slot + 1] == want, tile, code)
    codes[L_ROW : L_ROW + 8, :] = code
    codes[C_ROW : C_ROW + 8, :] = jnp.zeros((8, 256), jnp.int32)
    spot = ci_ref[...] - 4 * base_quad
    codes[C_ROW : C_ROW + 8, 0 : spot.shape[1]] = jnp.where((spot >= 0) & (spot < 4 * QUADS), spot, 4 * QUADS)
    down_copy = pltpu.make_async_copy(codes, spots, in_sem.at[8])
    down_copy.start()

    @pl.loop(0, 2 * QUADS + 1)
    def _(q):
        total[q] = jnp.zeros(total.shape[1:], jnp.float32)

    table[ZERO_S] = jnp.zeros((B, 128), jnp.bfloat16)
    l_table[ZERO_L] = jnp.zeros((B, 128), jnp.bfloat16)
    down_copy.wait()
    l_in.wait()

    @pl.loop(0, 8)
    def _(i):
        for t in range(15):
            v = l_ref[i, :, t * 128 : t * 128 + 128]
            l_table[t] = v
            l_table[15 + t] = swap(v)
        rows = pl.ds(pl.multiple_of(i * B, B), B)
        for g in range(VIEW):
            for at in range(4):
                spot = 8 * g + 2 * at
                dense_l[g, rows, at * 128 : at * 128 + 128] = jnp.where(
                    low16, l_table[spots[L_ROW + i, spot]], l_table[spots[L_ROW + i, spot + 1]]
                )

    def multiply(chunk, half, quad=None):
        view = chunk - skip
        if quad is None:
            near_rows, tile_count, tile_first = 8, TILES, 0
            left = dense_l.at[view]
        else:
            near_rows, tile_count, tile_first = 4, PIECE, PIECE * quad
            left = dense_l.at[view, :, pl.ds(pl.multiple_of(4 * B * quad, 4 * B), 4 * B)]
        depth = slice(0, near_rows * B)

        @pl.loop(0, 2)
        def _(p):
            for t in range(tile_count):
                at = tile_first + t
                v = near[chunk, 2 * half + p, at]
                table[p * TILES + at] = v
                table[40 + p * TILES + at] = swap(v)

        start = jnp.clip(first_quad + 2 * view - 3, 0, quad_count - SPAN) - base_quad
        first = 4 * first_quad - base_row + view * 8 + (0 if quad is None else 4 * quad)

        for n in range(4):
            for row in range(near_rows):
                for w in range(2):
                    spot = 8 * n + 4 * w + 2 * half
                    dense_s[n, row * B : row * B + B, w * 128 : w * 128 + 128] = jnp.where(
                        low16, table[spots[spot, first + row]], table[spots[spot + 1, first + row]]
                    )
            part = jnp.dot(left[...], dense_s[n, depth, :], preferred_element_type=jnp.float32)
            at = 2 * (start + 2 * n) + half
            total[at] += part[:, :128]
            total[at + 2] += part[:, 128:]

    events = ("A0", "A1", "X0", "C0", "A2", "X1", "C1", "A3", "E0", "X2")

    def when_prev(action):
        pl.when(has_prev)(action)

    def used(order):
        return jnp.where(outer, order != 0, order != 5) & (has_prev | (order < 4))

    def arrive_x(s):
        x_copy(s).wait_recv()
        if s < 2:
            for piece in pieces(s, 1):
                pl.when(has_next)(lambda: e_copy(s, piece).start())
                x_copy(s + 2, piece).start()
        d_copy(s).start()

    def arrive_c(s):
        c_copy(s).wait_recv()
        f_copy(s).start()

    def arrive_e(s):
        e_copy(s).wait_recv()
        g_copy(s).start()

    def before(kind, s):
        if kind == "A":
            a_copy(s).wait_recv()
        elif kind == "X":
            if s < 2:
                arrive_x(s)
                if s == 0:
                    when_prev(lambda: arrive_c(0))
            d_copy(s).wait_recv()
        elif kind == "C":
            if s == 0:
                when_prev(lambda: f_copy(0).wait_recv())
            else:

                @pl.when(has_prev & outer_core)
                def _():
                    c_copy(1).wait_recv()
                    f_copy(1).wait_recv()

        else:
            when_prev(lambda: arrive_e(s))
            arrive_x(2)
            when_prev(lambda: g_copy(s).wait_recv())

    @pl.loop(0, len(events))
    def _(e):
        order, own_half = e * 0, e * 0
        for index, (kind, s) in enumerate(events):
            order = jnp.where(e == index, int(s) if kind in "AX" else 4 + int(s), order)
            own_half = jnp.where(e == index, 1 if kind in "AC" else 0, own_half)
            pl.when(e == index)(functools.partial(before, kind, int(s)))

        @pl.when(used(order))
        def _():
            multiply(flip(order), jnp.where(own_half == 1, x, 1 - x))

    def pick(half):
        @pl.loop(0, 8)
        def _(i):
            rows = pl.ds(pl.multiple_of(i * B, B), B)
            for m in range(6):
                slot = 12 * half + 2 * m
                left, right = spots[C_ROW + i, slot], spots[C_ROW + i, slot + 1]
                a, b = total[left // 2, rows, :], total[right // 2, rows, :]
                straight = jnp.where(low, a, b)
                crossed = pltpu.roll(jnp.where(low, b, a), B, 1)
                keep = jnp.where(low, 1 - left % 2, right % 2) == 1
                at = pl.ds(pl.multiple_of(slot * B, 2 * B), 2 * B)
                out_ref[i, :, at] = jnp.where(keep, straight, crossed).astype(jnp.bfloat16)

    pick(x)

    for piece in range(2):
        x_copy(3, piece).wait_recv()
        d_copy(3, piece).start()

        def halo_piece():
            e_copy(1, piece).wait_recv()
            g_copy(1, piece).wait_recv()

        @pl.loop(0, 2)
        def _(e):
            pl.when((e == 0) & has_prev & outer_core)(halo_piece)
            pl.when(e == 1)(lambda: d_copy(3, piece).wait_recv())
            order = 5 - 2 * e

            @pl.when(used(order))
            def _():
                multiply(flip(order), 1 - x, 1 - x if piece == 0 else x)

    pick(1 - x)

    for s in range(4):
        a_copy(s).wait_send()
        for piece in pieces(s, 3):
            x_copy(s, piece).wait_send()
            d_copy(s, piece).wait_send()
    for s in range(2):

        @pl.when(has_next)
        def _():
            c_copy(s).wait_send()
            for piece in pieces(s, 1):
                e_copy(s, piece).wait_send()

        @pl.when(has_prev)
        def _():
            if s == 0:
                f_copy(s).wait_send()
                g_copy(s).wait_send()


def shards(l_blocks, s_blocks, l_index, s_cols, c_index):
    row_count = lax.axis_size("rows")
    own, kept = l_blocks.shape[0], c_index.shape[1]
    vmem, hbm = pl.BlockSpec(memory_space=pltpu.VMEM), pl.BlockSpec(memory_space=pl.ANY)
    return pl.pallas_call(
        functools.partial(kernel, row_count),
        out_shape=pltpu.VMEM((own, B, kept * B), jnp.bfloat16),
        in_specs=[hbm] * 5,
        out_specs=vmem,
        scratch_shapes=[
            pltpu.VMEM(s_blocks.shape, jnp.bfloat16),
            pltpu.VMEM(l_blocks.shape, jnp.bfloat16),
            pltpu.VMEM(l_index.shape, jnp.int32),
            pltpu.VMEM(s_cols.shape[::-1], jnp.int32),
            pltpu.VMEM(c_index.shape, jnp.int32),
            pltpu.VMEM((CHUNKS, PARTS, TILES, B, 128), jnp.bfloat16),
            pltpu.VMEM((ZERO_S + 1, B, 128), jnp.bfloat16),
            pltpu.VMEM((4, 8 * B, 4 * B), jnp.bfloat16),
            pltpu.VMEM((ZERO_L + 1, B, 128), jnp.bfloat16),
            pltpu.VMEM((VIEW, own * B, 8 * B), jnp.bfloat16),
            pltpu.VMEM((2 * QUADS + 1, own * B, 128), jnp.float32),
            pltpu.VMEM((C_ROW + 8, 256), jnp.int32),
            pltpu.SMEM((C_ROW + 8, 256), jnp.int32),
            pltpu.SemaphoreType.DMA((LATE + 5,)),
            pltpu.SemaphoreType.DMA((LATE + 5,)),
            pltpu.SemaphoreType.DMA((9,)),
        ],
        compiler_params=pltpu.CompilerParams(
            collective_id=0, has_side_effects=True, vmem_limit_bytes=56 * 1024 * 1024
        ),
        cost_estimate=pl.CostEstimate(flops=4_700_000_000, bytes_accessed=5_000_000, transcendentals=0),
    )(s_blocks, l_blocks, l_index, s_cols.T, c_index)


def solution(mesh):
    return jax.shard_map(
        shards,
        mesh=mesh,
        in_specs=(
            P(("rows", "cols"), None, None),
            P("rows", None, "cols"),
            P(("rows", "cols"), None),
            P(),
            P(("rows", "cols"), None),
        ),
        out_specs=P(("rows", "cols"), None, None),
        check_vma=False,
    )
```

```python
import functools

import jax
import jax.numpy as jnp
from jax import lax
from jax.experimental import pallas as pl
from jax.experimental.pallas import tpu as pltpu
from jax.sharding import PartitionSpec as P

MESH = pl.DeviceIdType.MESH
B = 64
PARTS = 4
KSP = 5
SPAN = 8
TILES = 20
CHUNKS = 6
QUADS = 16
VIEW = 5
ZERO_S = 80
ZERO_L = 30
L_ROW, C_ROW = 32, 40
X0, A0, C0, E0, D0, F0, G0 = 0, 4, 8, 10, 12, 16, 18
LATE = 20
PIECE = TILES // 2


def place(row_count):
    r = lax.axis_index("rows")
    c = lax.axis_index("cols")
    x = c // 2
    outer = jnp.where(x == 0, (c == 0) & (r > 0), (c == 3) & (r < row_count - 1))
    skip = jnp.where(x == 0, jnp.where(outer, 0, 1), jnp.where(outer, 1, 0))
    first_quad = 8 * r - 4 * (1 - x) + 2 * skip
    return r, c, x, outer, skip, first_quad


def swap(v):
    return jnp.concatenate([v[:, B:], v[:, :B]], axis=1)


def kernel(
    row_count, s_hbm, l_hbm, li_hbm, sc_hbm, ci_hbm, out_ref,
    s_ref, l_ref, li_ref, sc_ref, ci_ref, near, table, dense_s, l_table, dense_l, total, codes, spots,
    send_sem, recv_sem, in_sem,
):
    r, c, x, outer, skip, first_quad = place(row_count)
    k = c % 2
    up, down = r < row_count - 1, r > 0
    has_next = jnp.where(x == 0, up, down)
    has_prev = jnp.where(x == 0, down, up)
    next_row = jnp.where(x == 0, r + 1, r - 1)
    core = (r, 2 * x + 1 - k)
    across = (r, 2 * (1 - x) + k)
    ahead = (next_row, c)
    ahead_outer = (next_row, 3 * x)
    outer_core = k == x
    mine, theirs = c, 2 * (1 - x) + k
    quad_count = 8 * row_count
    base_quad = jnp.clip(first_quad - 3, 0, quad_count - QUADS)

    barrier = pltpu.get_barrier_semaphore()
    pl.semaphore_signal(barrier, inc=1, device_id=core, device_id_type=MESH)
    pl.semaphore_signal(barrier, inc=1, device_id=across, device_id_type=MESH)

    @pl.when(up)
    def _():
        pl.semaphore_signal(barrier, inc=1, device_id=(r + 1, c), device_id_type=MESH)
        pl.semaphore_signal(barrier, inc=1, device_id=(r + 1, 2 * x + 1 - k), device_id_type=MESH)

    @pl.when(down)
    def _():
        pl.semaphore_signal(barrier, inc=1, device_id=(r - 1, c), device_id_type=MESH)
        pl.semaphore_signal(barrier, inc=1, device_id=(r - 1, 2 * x + 1 - k), device_id_type=MESH)

    def s_in(step):
        rows = pl.ds(8 * jnp.where(x == 0, step, 3 - step), 8)
        return pltpu.make_async_copy(s_hbm.at[rows], s_ref.at[rows], in_sem.at[step])

    for step in (0, 3, 1, 2):
        s_in(step).start()
    small_in = [
        pltpu.make_async_copy(source, target, in_sem.at[4 + n])
        for n, (source, target) in enumerate(((sc_hbm, sc_ref), (li_hbm, li_ref), (ci_hbm, ci_ref), (l_hbm, l_ref)))
    ]
    l_in = small_in.pop()
    for operand in small_in:
        operand.start()
    l_in.start()

    low = lax.broadcasted_iota(jnp.int32, (B, 128), 1) < B
    low16 = lax.broadcasted_iota(jnp.int16, (B, 128), 1) < B

    def flip(t):
        return jnp.where(x == 1, t, 5 - t)

    def copy(src_chunk, dst_chunk, part, index, device, piece=None, trim=False, near_quad=1 - x):
        if piece is None:
            tiles = pl.ds(2 * (1 - x), TILES - 2) if trim else slice(None)
        elif piece == 0:
            tiles = pl.ds(PIECE * near_quad, PIECE)
        else:
            tiles = pl.ds(2 + 8 * x, PIECE - 2) if trim else pl.ds(PIECE * (1 - near_quad), PIECE)
        index = LATE + (index - X0) // 4 if piece else index
        return pltpu.make_async_remote_copy(
            src_ref=near.at[src_chunk, part, tiles],
            dst_ref=near.at[dst_chunk, part, tiles],
            send_sem=send_sem.at[index],
            recv_sem=recv_sem.at[index],
            device_id=device,
            device_id_type=MESH,
        )

    def x_copy(s, piece=None):
        source, target = jnp.where(x == 0, s + 2, 3 - s), jnp.where(x == 0, s, 5 - s)
        return copy(source, target, mine, X0 + s, across, piece, near_quad=x)

    def a_copy(s):
        return copy(flip(s), flip(s), mine, A0 + s, core)

    def c_copy(s):
        if s == 1:
            return copy(flip(1), flip(5), mine, jnp.where(outer_core, C0 + 1, F0 + 1), ahead_outer, trim=True)
        return copy(flip(s), flip(4 + s), mine, C0 + s, ahead)

    def e_copy(s, piece=None):
        if s == 1:
            index = jnp.where(outer_core, E0 + 1, G0 + 1)
            return copy(flip(1), flip(5), theirs, index, ahead_outer, piece, trim=True)
        return copy(flip(s), flip(4 + s), theirs, E0 + s, ahead)

    def d_copy(s, piece=None):
        return copy(flip(s), flip(s), theirs, D0 + s, core, piece)

    def f_copy(s):
        return copy(flip(4 + s), flip(4 + s), mine, F0 + s, core, trim=s == 1)

    def g_copy(s, piece=None):
        return copy(flip(4 + s), flip(4 + s), theirs, G0 + s, core, piece, trim=s == 1)

    def pieces(s, last):
        return (0, 1) if s == last else (None,)

    for step in (0, 3, 1, 2):
        group_chunk = jnp.where(x == 0, step, 3 - step)
        chunk = group_chunk + 2 * (1 - x)
        s_in(step).wait()

        @pl.loop(0, 4)
        def _(pair):
            at = pair * 5
            source = 8 * group_chunk + 2 * pair
            for odd in range(2):
                for t in range(2):
                    near[chunk, mine, at + 3 * odd + t] = s_ref[source + odd, :, t * 128 : t * 128 + 128]
            near[chunk, mine, at + 2] = jnp.concatenate(
                [s_ref[source, :, 256:320], s_ref[source + 1, :, 256:320]], axis=1
            )

        if step == 0:
            pl.semaphore_wait(barrier, 2 + 2 * up.astype(jnp.int32) + 2 * down.astype(jnp.int32))
        if step < 2:
            x_copy(step).start()
        else:

            @pl.when(has_next)
            def _():
                c_copy(3 - step).start()

        a_copy(3 - step).start()

    for operand in small_in:
        operand.wait()
    base_row = 128 * jnp.clip(4 * first_quad // 128, 0, 4 * quad_count // 128 - 2)
    cols = sc_ref[:, pl.ds(pl.multiple_of(base_row, 128), 256)]
    want_at = lax.broadcasted_iota(jnp.int32, (4 * SPAN, 256), 0)
    row = lax.broadcasted_iota(jnp.int32, (4 * SPAN, 256), 1)
    odd, side = row % 2, want_at % 2
    want = 4 * jnp.clip(2 * ((base_row + row) // 8) - 3, 0, quad_count - SPAN) + want_at
    want = jnp.where(base_row + row == 32 * r + jnp.where(x == 0, -16, 47), -1, want)
    first_tile = ((row // 2) % 4) * 5
    code = jnp.full((4 * SPAN, 256), ZERO_S, jnp.int32)
    for within in range(KSP):
        if within < 4:
            tile = first_tile + 3 * odd + within // 2 + jnp.where(side != within % 2, 40, 0)
        else:
            tile = first_tile + 2 + jnp.where(side != odd, 40, 0)
        for part in range(PARTS):
            slot = part * KSP + within
            code = jnp.where(cols[slot : slot + 1, :] == want, tile + (part % 2) * TILES, code)
    codes[0 : 4 * SPAN, :] = code
    lane = lax.broadcasted_iota(jnp.int32, (8, 256), 1)
    side = lane % 2
    want = jnp.where(lane < 8 * VIEW, 4 * first_quad + lane, -1)
    code = jnp.full((8, 256), ZERO_L, jnp.int32)
    for slot in range(30):
        tile = slot // 2 + jnp.where(side != slot % 2, 15, 0)
        code = jnp.where(li_ref[:, slot : slot + 1] == want, tile, code)
    codes[L_ROW : L_ROW + 8, :] = code
    codes[C_ROW : C_ROW + 8, :] = jnp.zeros((8, 256), jnp.int32)
    spot = ci_ref[...] - 4 * base_quad
    codes[C_ROW : C_ROW + 8, 0 : spot.shape[1]] = jnp.where((spot >= 0) & (spot < 4 * QUADS), spot, 4 * QUADS)
    down_copy = pltpu.make_async_copy(codes, spots, in_sem.at[8])
    down_copy.start()

    @pl.loop(0, 2 * QUADS + 1)
    def _(q):
        total[q] = jnp.zeros(total.shape[1:], jnp.float32)

    table[ZERO_S] = jnp.zeros((B, 128), jnp.bfloat16)
    l_table[ZERO_L] = jnp.zeros((B, 128), jnp.bfloat16)
    down_copy.wait()
    l_in.wait()

    @pl.loop(0, 8)
    def _(i):
        for t in range(15):
            v = l_ref[i, :, t * 128 : t * 128 + 128]
            l_table[t] = v
            l_table[15 + t] = swap(v)
        rows = pl.ds(pl.multiple_of(i * B, B), B)
        for g in range(VIEW):
            for at in range(4):
                spot = 8 * g + 2 * at
                dense_l[g, rows, at * 128 : at * 128 + 128] = jnp.where(
                    low16, l_table[spots[L_ROW + i, spot]], l_table[spots[L_ROW + i, spot + 1]]
                )

    def multiply(chunk, half, quad=None):
        view = chunk - skip
        if quad is None:
            near_rows, tile_count, tile_first = 8, TILES, 0
            left = dense_l.at[view]
        else:
            near_rows, tile_count, tile_first = 4, PIECE, PIECE * quad
            left = dense_l.at[view, :, pl.ds(pl.multiple_of(4 * B * quad, 4 * B), 4 * B)]
        depth = slice(0, near_rows * B)

        @pl.loop(0, 2)
        def _(p):
            for t in range(tile_count):
                at = tile_first + t
                v = near[chunk, 2 * half + p, at]
                table[p * TILES + at] = v
                table[40 + p * TILES + at] = swap(v)

        start = jnp.clip(first_quad + 2 * view - 3, 0, quad_count - SPAN) - base_quad
        first = 4 * first_quad - base_row + view * 8 + (0 if quad is None else 4 * quad)

        for n in range(4):
            for row in range(near_rows):
                for w in range(2):
                    spot = 8 * n + 4 * w + 2 * half
                    dense_s[n, row * B : row * B + B, w * 128 : w * 128 + 128] = jnp.where(
                        low16, table[spots[spot, first + row]], table[spots[spot + 1, first + row]]
                    )
            part = jnp.dot(left[...], dense_s[n, depth, :], preferred_element_type=jnp.float32)
            at = 2 * (start + 2 * n) + half
            total[at] += part[:, :128]
            total[at + 2] += part[:, 128:]

    events = ("A0", "A1", "A2", "X0", "C0", "A3", "X1", "C1", "E0", "X2")

    def when_prev(action):
        pl.when(has_prev)(action)

    def used(order):
        return jnp.where(outer, order != 0, order != 5) & (has_prev | (order < 4))

    def arrive_x(s):
        x_copy(s).wait_recv()
        if s < 2:
            for piece in pieces(s, 1):
                pl.when(has_next)(lambda: e_copy(s, piece).start())
                x_copy(s + 2, piece).start()
        d_copy(s).start()

    def arrive_c(s):
        c_copy(s).wait_recv()
        f_copy(s).start()

    def arrive_e(s):
        e_copy(s).wait_recv()
        g_copy(s).start()

    def before(kind, s):
        if kind == "A":
            a_copy(s).wait_recv()
        elif kind == "X":
            if s < 2:
                arrive_x(s)
                if s == 0:
                    when_prev(lambda: arrive_c(0))
            d_copy(s).wait_recv()
        elif kind == "C":
            if s == 0:
                when_prev(lambda: f_copy(0).wait_recv())
            else:

                @pl.when(has_prev & outer_core)
                def _():
                    c_copy(1).wait_recv()
                    f_copy(1).wait_recv()

        else:
            when_prev(lambda: arrive_e(s))
            arrive_x(2)
            when_prev(lambda: g_copy(s).wait_recv())

    @pl.loop(0, len(events))
    def _(e):
        order, own_half = e * 0, e * 0
        for index, (kind, s) in enumerate(events):
            order = jnp.where(e == index, int(s) if kind in "AX" else 4 + int(s), order)
            own_half = jnp.where(e == index, 1 if kind in "AC" else 0, own_half)
            pl.when(e == index)(functools.partial(before, kind, int(s)))

        @pl.when(used(order))
        def _():
            multiply(flip(order), jnp.where(own_half == 1, x, 1 - x))

    def pick(half):
        @pl.loop(0, 8)
        def _(i):
            rows = pl.ds(pl.multiple_of(i * B, B), B)
            for m in range(6):
                slot = 12 * half + 2 * m
                left, right = spots[C_ROW + i, slot], spots[C_ROW + i, slot + 1]
                a, b = total[left // 2, rows, :], total[right // 2, rows, :]
                straight = jnp.where(low, a, b)
                crossed = pltpu.roll(jnp.where(low, b, a), B, 1)
                keep = jnp.where(low, 1 - left % 2, right % 2) == 1
                at = pl.ds(pl.multiple_of(slot * B, 2 * B), 2 * B)
                out_ref[i, :, at] = jnp.where(keep, straight, crossed).astype(jnp.bfloat16)

    for piece in range(2):
        x_copy(3, piece).wait_recv()
        d_copy(3, piece).start()

        def halo_piece():
            e_copy(1, piece).wait_recv()
            g_copy(1, piece).wait_recv()

        @pl.loop(0, 2)
        def _(e):
            pl.when((e == 0) & has_prev & outer_core)(halo_piece)
            pl.when(e == 1)(lambda: d_copy(3, piece).wait_recv())
            order = 5 - 2 * e

            @pl.when(used(order))
            def _():
                multiply(flip(order), 1 - x, 1 - x if piece == 0 else x)

        pick(x if piece == 0 else 1 - x)

    for s in range(4):
        a_copy(s).wait_send()
        for piece in pieces(s, 3):
            x_copy(s, piece).wait_send()
            d_copy(s, piece).wait_send()
    for s in range(2):

        @pl.when(has_next)
        def _():
            c_copy(s).wait_send()
            for piece in pieces(s, 1):
                e_copy(s, piece).wait_send()

        @pl.when(has_prev)
        def _():
            if s == 0:
                f_copy(s).wait_send()
                g_copy(s).wait_send()


def shards(l_blocks, s_blocks, l_index, s_cols, c_index):
    row_count = lax.axis_size("rows")
    own, kept = l_blocks.shape[0], c_index.shape[1]
    vmem, hbm = pl.BlockSpec(memory_space=pltpu.VMEM), pl.BlockSpec(memory_space=pl.ANY)
    return pl.pallas_call(
        functools.partial(kernel, row_count),
        out_shape=pltpu.VMEM((own, B, kept * B), jnp.bfloat16),
        in_specs=[hbm] * 5,
        out_specs=vmem,
        scratch_shapes=[
            pltpu.VMEM(s_blocks.shape, jnp.bfloat16),
            pltpu.VMEM(l_blocks.shape, jnp.bfloat16),
            pltpu.VMEM(l_index.shape, jnp.int32),
            pltpu.VMEM(s_cols.shape[::-1], jnp.int32),
            pltpu.VMEM(c_index.shape, jnp.int32),
            pltpu.VMEM((CHUNKS, PARTS, TILES, B, 128), jnp.bfloat16),
            pltpu.VMEM((ZERO_S + 1, B, 128), jnp.bfloat16),
            pltpu.VMEM((4, 8 * B, 4 * B), jnp.bfloat16),
            pltpu.VMEM((ZERO_L + 1, B, 128), jnp.bfloat16),
            pltpu.VMEM((VIEW, own * B, 8 * B), jnp.bfloat16),
            pltpu.VMEM((2 * QUADS + 1, own * B, 128), jnp.float32),
            pltpu.VMEM((C_ROW + 8, 256), jnp.int32),
            pltpu.SMEM((C_ROW + 8, 256), jnp.int32),
            pltpu.SemaphoreType.DMA((LATE + 5,)),
            pltpu.SemaphoreType.DMA((LATE + 5,)),
            pltpu.SemaphoreType.DMA((9,)),
        ],
        compiler_params=pltpu.CompilerParams(
            collective_id=0, has_side_effects=True, vmem_limit_bytes=56 * 1024 * 1024
        ),
        cost_estimate=pl.CostEstimate(flops=4_700_000_000, bytes_accessed=5_000_000, transcendentals=0),
    )(s_blocks, l_blocks, l_index, s_cols.T, c_index)


def solution(mesh):
    return jax.shard_map(
        shards,
        mesh=mesh,
        in_specs=(
            P(("rows", "cols"), None, None),
            P("rows", None, "cols"),
            P(("rows", "cols"), None),
            P(),
            P(("rows", "cols"), None),
        ),
        out_specs=P(("rows", "cols"), None, None),
        check_vma=False,
    )
```
